512 devices in a mesh: blk: 128 (over z, y, core), dp: 4 (over x).
Axes of the slice: x: 4, y: 8, z: 8, core: 2. Of those that a mesh axis runs over, the one named last changes fastest.
Arguments:
- features: bfloat16 [4, 32768, 128], P('dp', 'blk'), may hold values from -6 to 6
- kernel_map: int32 [4, 27, 32768], P('dp', None, 'blk'), may hold values from -1 to 128, as said below
- block_counts: int32 [4, 128], P('dp'), may hold values from 128 to 256, as said below
- send_position: int32 [4, 32768], P('dp', 'blk'), may hold values from 0 to 511, as said below
- cell_source: int32 [4, 65536], P('dp', 'blk'), may hold values from 0 to 511, as said below
- conv_weight: bfloat16 [27, 128, 128], replicated, may hold values from -0.109375 to 0.109375
- down_weight: bfloat16 [1024, 256], replicated, may hold values from -0.1875 to 0.1875
- cotangent: bfloat16 [4, 8192, 256], P('dp', 'blk'), may hold values from -0.023925781 to 0.023925781
Outputs:
- coarse: bfloat16 [4, 8192, 256], P('dp', 'blk')
- grad_conv: float32 [27, 128, 128], replicated
- grad_down: float32 [1024, 256], replicated
The draws below stay inside these ranges and needn't reach their ends.
Inputs may be any that keep to these rules, and one draw needn't show every extreme that they name: `kernel_map`: where an entry is not -1, row g + entry - 64 lies within the same scene; offset 27 // 2 has the entry 64 for every row. `block_counts`: every scene has a block with all 256 rows occupied. `send_position`: within one block's rows the entries are distinct, and no owner (entry // 4) is named by more than 4 of them; some owner is named exactly 4 times in every block. `cell_source`: the entries of one owner's 8 * 64 positions are a permutation.
All inputs are finite; a program needn't handle non-finite values.
Results may differ from the reference program's by a relative error of at most 0.005.
Values may be sent and summed in bfloat16 or wider, within the bound.
A program may use at most 64 MiB of HBM per device.

```python
import jax
import jax.numpy as jnp
from jax import lax

C = 128
C2 = 256
KOFF = 27
OCT = 8
ROWS = 256
HALO = 64
CAP = 4
CROWS = 64
SCENES = 4
VOX = 32768
CVOX = 8192
N_BLK = 128


def draw_kernel_map(key, part):
    key = jax.random.fold_in(key, 11)
    first_key, second_key = jax.random.split(key)
    shape = (SCENES, KOFF, VOX)
    rows = jnp.arange(VOX, dtype=jnp.int32)[None, None, :]
    delta = jax.random.randint(first_key, shape, -HALO, HALO + 1)
    keep = jax.random.randint(second_key, shape, 0, 10) < 7
    offset = jnp.arange(KOFF, dtype=jnp.int32)[None, :, None]
    center = offset == KOFF // 2
    delta = jnp.where(center, 0, delta)
    source = rows + delta
    valid = (center | keep) & (source >= 0) & (source < VOX)
    valid = valid & jnp.logical_not((offset == 0) & (rows == 0))
    return jnp.where(valid, delta + HALO, -1).astype(jnp.int32)


def draw_block_counts(key, part):
    key = jax.random.fold_in(key, 12)
    first_key, second_key = jax.random.split(key)
    counts = jax.random.randint(first_key, (SCENES, N_BLK), ROWS // 2, ROWS + 1)
    full = jax.random.randint(second_key, (SCENES, 1), 0, N_BLK)
    return jnp.where(jnp.arange(N_BLK)[None, :] == full, ROWS, counts).astype(jnp.int32)


def block_positions(key):
    first_key, second_key, third_key = jax.random.split(key, 3)
    chosen = jax.random.randint(first_key, (), 0, N_BLK)
    others = jax.random.permutation(second_key, (N_BLK - 1) * CAP)
    others = others + CAP * (others // CAP >= chosen).astype(others.dtype)
    placed = jnp.concatenate([chosen * CAP + jnp.arange(CAP, dtype=others.dtype), others[:ROWS - CAP]])
    return jax.random.permutation(third_key, placed)


def draw_send_position(key, part):
    key = jax.random.fold_in(key, 13)
    keys = jax.random.split(key, SCENES * N_BLK)
    return jax.vmap(block_positions)(keys).reshape(SCENES, VOX).astype(jnp.int32)


def owner_cells(key):
    return jax.random.permutation(key, 2 * ROWS)


def draw_cell_source(key, part):
    key = jax.random.fold_in(key, 14)
    keys = jax.random.split(key, SCENES * N_BLK)
    return jax.vmap(owner_cells)(keys).reshape(SCENES, OCT * CVOX).astype(jnp.int32)


def steps_of(rng, extent, cuts, least, largest):
    loudness, own = 1.0, jax.random.fold_in(rng, 6)
    for position, blocks in cuts:
        heights = jnp.exp(jax.random.uniform(jax.random.fold_in(own, position), (blocks,), jnp.float32, least / len(cuts), largest / len(cuts)))
        loudness = loudness * jnp.repeat(heights, extent[position] // blocks).reshape([-1 if axis == position else 1 for axis in range(len(extent))])
    return loudness


def scatter_about(stream_key, dims, scale, limit, cuts=(), kind=jnp.bfloat16):
    result = scale * jax.random.normal(stream_key, dims, jnp.float32)
    if cuts:
        result = result * steps_of(stream_key, dims, cuts, -0.22, 0.18)
    return jnp.clip(result, -limit, limit).astype(kind)


def setup_inputs(seed: int = 0) -> dict:
    splits = jax.random.split(jax.random.key(seed), 9)
    features = scatter_about(splits[0], (SCENES, VOX, C), 1.0, 6.0, ((0, 4), (1, 128)))
    kernel_map = draw_kernel_map(jax.random.fold_in(splits[8], 71), 0)
    block_counts = draw_block_counts(jax.random.fold_in(splits[8], 71), 0)
    send_position = draw_send_position(jax.random.fold_in(splits[8], 71), 0)
    cell_source = draw_cell_source(jax.random.fold_in(splits[8], 71), 0)
    conv_weight = scatter_about(splits[5], (KOFF, C, C), (KOFF * C) ** -0.5, 0.109375)
    down_weight = scatter_about(splits[6], (OCT * C, C2), (OCT * C) ** -0.5, 0.1875)
    cotangent = scatter_about(splits[7], (SCENES, CVOX, C2), 0.004, 0.023925781, ((0, 4), (1, 128)))
    return {"features": features, "kernel_map": kernel_map, "block_counts": block_counts, "send_position": send_position, "cell_source": cell_source, "conv_weight": conv_weight, "down_weight": down_weight, "cotangent": cotangent}


def silu_grad(pre):
    sig = jax.nn.sigmoid(pre)
    return sig * (1.0 + pre * (1.0 - sig))

def reference(features, kernel_map, block_counts, send_position, cell_source, conv_weight, down_weight, cotangent):
    rows_all = jnp.arange(VOX, dtype=jnp.int32)
    coarse_list = []
    grad_conv = jnp.zeros((KOFF, C, C), jnp.float32)
    grad_down = jnp.zeros((OCT * C, C2), jnp.float32)
    for scene in range(SCENES):
        inside = rows_all % ROWS
        counted = block_counts[scene][rows_all // ROWS]
        live = (inside < counted // 2) | (inside >= ROWS - (counted - counted // 2))
        masked = jnp.where(live[:, None], features[scene], jnp.zeros((), jnp.bfloat16))
        table = jnp.concatenate([masked, jnp.zeros((1, C), jnp.bfloat16)], 0)
        index = jnp.where(kernel_map[scene] >= 0, rows_all[None, :] + kernel_map[scene] - HALO, VOX).astype(jnp.int32)

        def forward_step(total, pair):
            index_row, weight = pair
            picked = jnp.take(table, index_row, axis=0)
            return (total + jnp.dot(picked, weight, preferred_element_type=jnp.float32), None)
        pre, _ = lax.scan(forward_step, jnp.zeros((VOX, C), jnp.float32), (index, conv_weight))
        hidden = (jax.nn.silu(pre) * live[:, None]).astype(jnp.bfloat16)
        owner = send_position[scene] // CAP
        slot = send_position[scene] % CAP
        cell = (owner * (2 * ROWS) + rows_all // ROWS * CAP + slot).astype(jnp.int32)
        cells = jnp.zeros((N_BLK * 2 * ROWS, C), jnp.bfloat16).at[cell].set(hidden)
        fetch = (jnp.arange(OCT * CVOX, dtype=jnp.int32) // (OCT * CROWS) * (2 * ROWS) + cell_source[scene]).astype(jnp.int32)
        grid = jnp.take(cells, fetch, axis=0).reshape(CVOX, OCT * C)
        coarse_list.append(jnp.dot(grid, down_weight, preferred_element_type=jnp.float32).astype(jnp.bfloat16))
        grad_down = grad_down + lax.dot_general(grid, cotangent[scene], (((0,), (0,)), ((), ())), preferred_element_type=jnp.float32)
        grad_grid = lax.dot_general(cotangent[scene], down_weight, (((1,), (1,)), ((), ())), preferred_element_type=jnp.float32).astype(jnp.bfloat16)
        returned = jnp.zeros((N_BLK * 2 * ROWS, C), jnp.bfloat16).at[fetch].set(grad_grid.reshape(OCT * CVOX, C))
        grad_hidden = jnp.take(returned, cell, axis=0)
        grad_pre = (grad_hidden.astype(jnp.float32) * silu_grad(pre) * live[:, None]).astype(jnp.bfloat16)

        def backward_step(carry, index_row):
            picked = jnp.take(table, index_row, axis=0)
            return (carry, lax.dot_general(picked, grad_pre, (((0,), (0,)), ((), ())), preferred_element_type=jnp.float32))
        _, scene_grad = lax.scan(backward_step, jnp.zeros((), jnp.float32), index)
        grad_conv = grad_conv + scene_grad
    return (jnp.stack(coarse_list, 0), grad_conv, grad_down)
```

```python
import functools
import math

import jax
import jax.numpy as jnp
from jax import lax
from jax.experimental import pallas as pl
from jax.experimental.pallas import tpu as pltpu
from jax.sharding import PartitionSpec as P

OCT = 8
HALO = 64
F32 = jnp.float32
BF16 = jnp.bfloat16
MESH = pl.DeviceIdType.MESH


def iota(shape, dim):
    return lax.broadcasted_iota(jnp.int32, shape, dim)


def dot(a, b, ca, cb):
    return lax.dot_general(a, b, (((ca,), (cb,)), ((), ())), preferred_element_type=F32)


def up16(rows):
    return -(-rows // 16) * 16


class Place:
    def __init__(self, n, nx):
        blk = lax.axis_index("blk")
        self.n, self.nx = n, nx
        self.blk, self.x = blk, lax.axis_index("dp")
        self.c = lax.rem(blk, 2)
        chip = lax.div(blk, 2)
        z, y = lax.div(chip, n), lax.rem(chip, n)
        self.a = (1 - self.c) * y + self.c * z
        self.b = (1 - self.c) * z + self.c * y

    def of(self, a, b):
        c, n = self.c, self.n
        return ((1 - c) * (b * n + a) + c * (a * n + b)) * 2 + c

    def along_a(self, p):
        return (self.of(lax.rem(self.a + p, self.n), self.b), self.x)

    def along_b(self, p):
        return (self.of(self.a, lax.rem(self.b + p, self.n)), self.x)

    def along_x(self, p):
        return (self.blk, lax.rem(self.x + p, self.nx))

    def other_core(self):
        return (self.blk + 1 - 2 * self.c, self.x)

    def next_block(self, p, count):
        return (lax.rem(self.blk + p, count), self.x)


class Sender:
    def __init__(self, send_sem, recv_sem):
        self.send_sem, self.recv_sem, self.used, self.all = send_sem, recv_sem, 0, []

    def start(self, src, dst, device):
        copy = pltpu.make_async_remote_copy(
            src_ref=src,
            dst_ref=dst,
            send_sem=self.send_sem.at[self.used],
            recv_sem=self.recv_sem.at[self.used],
            device_id=device,
            device_id_type=MESH,
        )
        self.used += 1
        copy.start()
        self.all.append(copy)
        return copy

    def finish(self):
        for copy in self.all:
            copy.wait_send()


def arrived(copies):
    for copy in copies:
        copy.wait_recv()


class Exchange:
    def __init__(self, place, sender, bufs):
        self.place, self.sender = place, sender
        self.send1, self.recv1, self.send2, self.recv2, self.got = bufs

    def start(self, rows):
        pc, n = self.place, self.place.n
        self.send1[...] = rows.reshape(self.send1.shape)
        self.copies = [
            self.sender.start(
                self.send1.at[lax.rem(pc.a + p, n)], self.recv1.at[pc.a], pc.along_a(p)
            )
            for p in range(1, n)
        ]
        self.recv1[pc.a] = self.send1[pc.a]

    def second(self, swap):
        pc, n = self.place, self.place.n
        arrived(self.copies)
        flat = self.recv1[...].reshape(swap.shape[1], -1)
        moved = jnp.dot(swap[...], flat, preferred_element_type=F32).astype(BF16)
        self.send2[...] = moved.reshape(self.send2.shape)
        self.copies = [
            self.sender.start(
                self.send2.at[lax.rem(pc.b + p, n)], self.recv2.at[pc.b], pc.along_b(p)
            )
            for p in range(1, n)
        ]
        self.recv2[pc.b] = self.send2[pc.b]

    def third(self):
        pc = self.place
        arrived(self.copies)
        self.copies = [
            self.sender.start(self.recv2.at[:, 1 - pc.c], self.got.at[pc.c], pc.other_core())
        ]
        self.got[pc.c] = self.recv2[:, pc.c]

    def result(self):
        arrived(self.copies)
        flat = self.got[...]
        return flat.reshape(-1, flat.shape[-1])


class Sum:
    def __init__(self, place, sender, rows, bufs, out):
        self.place, self.sender, self.rows, self.out = place, sender, rows, out
        n = place.n
        self.part = up16(-(-rows // n))
        self.wide = up16(rows)
        self.s0, self.r0, self.own, self.s1, self.r1 = bufs[:5]
        self.s2, self.r2, self.s3, self.g2, self.g1 = bufs[5:]

    @staticmethod
    def scratch(rows, n, nx):
        part, wide = up16(-(-rows // n)), up16(rows)
        return [
            pltpu.VMEM((n * rows, 128), BF16),
            pltpu.VMEM((n * rows, 128), BF16),
            pltpu.VMEM((n * rows, 128), F32),
            pltpu.VMEM((n, wide, 128), BF16),
            pltpu.VMEM((n, wide, 128), BF16),
            pltpu.VMEM((n, part, 128), F32),
            pltpu.VMEM((n, part, 128), F32),
            pltpu.VMEM((nx, part, 128), F32),
            pltpu.VMEM((n * part, 128), BF16),
            pltpu.VMEM((n, wide, 128), BF16),
        ]

    def start(self, theirs, mine):
        self.s0[...] = theirs().astype(BF16)
        self.copies = [self.sender.start(self.s0, self.r0, self.place.other_core())]
        self.own[...] = mine()

    def along_a(self):
        pc, n, rows = self.place, self.place.n, self.rows
        arrived(self.copies)
        for q in range(n):
            chunk = pl.ds(q * rows, rows)
            total = self.own[chunk] + self.r0[chunk].astype(F32)
            self.own[chunk] = total
            self.s1[q, pl.ds(0, rows)] = total.astype(BF16)
            if self.wide > rows:
                self.s1[q, pl.ds(rows, self.wide - rows)] = jnp.zeros(
                    (self.wide - rows, 128), BF16
                )
        self.copies = [
            self.sender.start(
                self.s1.at[lax.rem(pc.a + p, n)], self.r1.at[p], pc.along_a(p)
            )
            for p in range(1, n)
        ]

    def along_b(self):
        pc, n, rows = self.place, self.place.n, self.rows
        arrived(self.copies)
        total = self.own[pl.ds(pl.multiple_of(pc.a * rows, 8), rows)]
        for p in range(1, n):
            total += self.r1[p][:rows].astype(F32)
        spare = n * self.part - rows
        if spare:
            total = jnp.concatenate([total, jnp.zeros((spare, 128), F32)], 0)
        self.s2[...] = total.reshape(self.s2.shape)
        self.copies = [
            self.sender.start(
                self.s2.at[lax.rem(pc.b + p, n)], self.r2.at[p], pc.along_b(p)
            )
            for p in range(1, n)
        ]

    def along_x(self):
        pc, n = self.place, self.place.n
        arrived(self.copies)
        total = self.s2[pc.b]
        for p in range(1, n):
            total += self.r2[p]
        self.s3[pc.x] = total
        self.copies = [
            self.sender.start(self.s3.at[pc.x], self.s3.at[pc.x], pc.along_x(p))
            for p in range(1, pc.nx)
        ]

    def back_b(self):
        pc, n = self.place, self.place.n
        arrived(self.copies)
        total = self.s3[0]
        for x in range(1, pc.nx):
            total += self.s3[x]
        mine = pl.ds(pl.multiple_of(pc.b * self.part, 16), self.part)
        self.g2[mine] = total.astype(BF16)
        self.copies = [
            self.sender.start(self.g2.at[mine], self.g2.at[mine], pc.along_b(p))
            for p in range(1, n)
        ]

    def back_a(self):
        pc, n = self.place, self.place.n
        arrived(self.copies)
        self.g1[pc.a] = self.g2[pl.ds(0, self.wide)]
        self.copies = [
            self.sender.start(self.g1.at[pc.a], self.g1.at[pc.a], pc.along_a(p))
            for p in range(1, n)
        ]

    def back_core(self, sem):
        pc = self.place
        arrived(self.copies)
        self.copies = [self.sender.start(self.g1, self.out.at[pc.c], pc.other_core())]
        self.kept = pltpu.make_async_copy(self.g1, self.out.at[pc.c], sem)
        self.kept.start()

    def result(self):
        arrived(self.copies)
        self.kept.wait()


def kernel(n, nx, cap, *refs):
    (
        features,
        kernel_map,
        block_counts,
        send_position,
        cell_source,
        conv_weight,
        down_weight,
        cotangent,
        coarse,
        out_conv,
        out_down,
        table,
        index,
        weight_t,
        picked,
        by_child,
        send_hot,
        swap,
        down_grad,
        *rest,
    ) = refs
    *rest, send_sem, recv_sem, local_sem = rest
    count = 2 * n * n
    offsets = conv_weight.shape[0]
    rows, width = features.shape[1], features.shape[2]
    cells = n * n * 2 * cap
    taps = offsets * width
    half = taps // 2
    pc = Place(n, nx)
    sender = Sender(send_sem, recv_sem)

    barrier = pltpu.get_barrier_semaphore()
    partners = [pc.along_a(p) for p in range(1, n)] + [pc.along_b(p) for p in range(1, n)]
    partners += [pc.along_x(p) for p in range(1, nx)]
    partners += [pc.other_core(), pc.next_block(1, count), pc.next_block(count - 1, count)]
    for device in partners:
        pl.semaphore_signal(barrier, inc=1, device_id=device, device_id_type=MESH)

    counted = block_counts[0, pc.blk]
    front = lax.div(counted, 2)
    back = rows - (counted - front)
    down = iota((rows, width), 0)
    live = (down < front) | (down >= back)
    across = iota((1, rows), 1)
    live_t = (across < front) | (across >= back)
    masked = jnp.where(live, features[0].astype(F32), 0.0)
    table[pl.ds(HALO, rows)] = masked.astype(BF16)
    pl.semaphore_wait(barrier, len(partners))

    halo = [
        sender.start(
            table.at[pl.ds(rows, HALO)], table.at[pl.ds(0, HALO)], pc.next_block(1, count)
        ),
        sender.start(
            table.at[pl.ds(HALO, HALO)],
            table.at[pl.ds(HALO + rows, HALO)],
            pc.next_block(count - 1, count),
        ),
    ]

    forward = Exchange(pc, sender, rest[0:5])
    backward = Exchange(pc, sender, rest[5:10])
    sum_conv = Sum(pc, sender, half // n, rest[10:20], out_conv)
    sum_down = Sum(pc, sender, OCT * width // n, rest[20:30], out_down)

    r = iota((cells, 1), 0)
    slot, r1 = lax.rem(r, cap), lax.div(r, cap)
    to_b, r2 = lax.rem(r1, n), lax.div(r1, n)
    to_c, to_a = lax.rem(r2, 2), lax.div(r2, 2)
    chip = jnp.where(pc.c == 0, to_b * n + to_a, to_a * n + to_b)
    goes_to = (chip * 2 + to_c) * cap + slot
    from_a, from_b, from_c = to_b, lax.rem(r2, n), lax.div(r2, n)
    chip = jnp.where(from_c == 0, from_b * n + from_a, from_a * n + from_b)
    comes_from = (chip * 2 + from_c) * cap + slot

    def hot(at, values):
        return jnp.where(at == values, 1.0, 0.0).astype(BF16)

    for j in range(OCT):
        part = dot(cotangent[0], down_weight[pl.ds(j * width, width)], 1, 1)
        by_child[pl.ds(j, rows // 4, stride=OCT)] = part.astype(BF16).astype(F32)
    children = cell_source[...]
    backward.start(
        jnp.dot(hot(goes_to, children), by_child[...].astype(BF16), preferred_element_type=F32)
        .astype(BF16)
    )

    swapped = ((to_b * 2 + to_c) * n + to_a) * cap + slot
    swap[...] = hot(swapped, iota((1, cells), 1))
    position = send_position[...]
    send_hot[...] = hot(goes_to, position)
    for k in range(offsets):
        weight_t[:, pl.ds(k * width, width)] = conv_weight[k].astype(F32).T.astype(BF16)
    entry = kernel_map[0]
    lane = lax.rem(iota(entry.shape, 1), 128)
    index[...] = jnp.where(entry >= 0, entry + lane, -1)

    arrived(halo)
    table_t = table[...].astype(F32).T.astype(BF16)
    window = iota((2 * HALO + 128, 128), 0)
    for k in range(offsets):
        for t in range(rows // 128):
            chosen = hot(window, index[pl.ds(k, 1), pl.ds(t * 128, 128)])
            got = jnp.dot(
                table_t[:, t * 128 : t * 128 + 128 + 2 * HALO], chosen, preferred_element_type=F32
            )
            picked[pl.ds(k * width, width), pl.ds(t * 128, 128)] = got.astype(BF16)

    backward.second(swap)
    pre = jnp.dot(weight_t[...], picked[...], preferred_element_type=F32)
    sig = 1.0 / (1.0 + jnp.exp(-pre))
    hidden = jnp.where(live_t, pre * sig, 0.0).astype(BF16)
    forward.start(dot(send_hot[...], hidden, 1, 1).astype(BF16))

    backward.third()
    from_owner = hot(comes_from, position)
    slope = jnp.where(live_t, sig * (1.0 + pre * (1.0 - sig)), 0.0)
    grad_hidden = dot(backward.result(), from_owner, 0, 0)
    grad_pre = (grad_hidden * slope).astype(BF16)

    def conv_half(h):
        chosen = picked[pl.ds(pl.multiple_of(h * half, 16), half)]
        return dot(chosen, grad_pre, 1, 1)

    sum_conv.start(lambda: conv_half(1 - pc.c), lambda: conv_half(pc.c))
    forward.second(swap)
    sum_conv.along_a()
    forward.third()

    to_child = hot(comes_from, children)
    by_child[...] = dot(to_child, forward.result(), 0, 0)
    total = jnp.zeros(coarse.shape[1:], F32)
    for j in range(OCT):
        child = by_child[pl.ds(j, rows // 4, stride=OCT)].astype(BF16)
        grad = dot(child, cotangent[0], 0, 0)
        for h in range(2):
            down_grad[h, pl.ds(j * width, width)] = grad[:, h * 128 : (h + 1) * 128]
        total += jnp.dot(
            child, down_weight[pl.ds(j * width, width)], preferred_element_type=F32
        )
    sum_down.start(lambda: down_grad[1 - pc.c], lambda: down_grad[pc.c])
    coarse[0] = total.astype(BF16)

    sum_conv.along_b()
    sum_down.along_a()
    sum_conv.along_x()
    sum_down.along_b()
    sum_conv.back_b()
    sum_down.along_x()
    sum_conv.back_a()
    sum_down.back_b()
    sum_conv.back_core(local_sem.at[0])
    sum_down.back_a()
    sum_down.back_core(local_sem.at[1])
    sum_conv.result()
    sum_down.result()
    sender.finish()


def body(n, nx, *args):
    features, kernel_map, _, _, cell_source, conv_weight, down_weight, cotangent = args
    rows, width = features.shape[1:]
    offsets = conv_weight.shape[0]
    cells = cell_source.shape[1]
    cap = cells // (2 * n * n)
    half = offsets * width // 2
    exchange = [
        pltpu.VMEM((n, cells // n, width), BF16),
        pltpu.VMEM((n, cells // n, width), BF16),
        pltpu.VMEM((n, 2, cells // n // 2, width), BF16),
        pltpu.VMEM((n, 2, cells // n // 2, width), BF16),
        pltpu.VMEM((2, n, cells // n // 2, width), BF16),
    ]
    copies = 2 + 2 * (2 * (n - 1) + 1) + 2 * (4 * (n - 1) + nx - 1 + 2)
    vmem = pl.BlockSpec(memory_space=pltpu.VMEM)
    conv_rows, down_rows = half // n, OCT * width // n
    coarse, conv, down = pl.pallas_call(
        functools.partial(kernel, n, nx, cap),
        out_shape=[
            jax.ShapeDtypeStruct(cotangent.shape, BF16),
            jax.ShapeDtypeStruct((2, n, up16(conv_rows), 128), BF16),
            jax.ShapeDtypeStruct((2, n, up16(down_rows), 128), BF16),
        ],
        in_specs=[vmem, vmem, pl.BlockSpec(memory_space=pltpu.SMEM)] + [vmem] * 5,
        out_specs=[vmem, pl.BlockSpec(memory_space=pl.ANY), pl.BlockSpec(memory_space=pl.ANY)],
        scratch_shapes=[
            pltpu.VMEM((rows + 2 * HALO, width), BF16),
            pltpu.VMEM((offsets, rows), jnp.int32),
            pltpu.VMEM((width, offsets * width), BF16),
            pltpu.VMEM((offsets * width, rows), BF16),
            pltpu.VMEM((cells, width), F32),
            pltpu.VMEM((cells, rows), BF16),
            pltpu.VMEM((cells, cells), BF16),
            pltpu.VMEM((2, OCT * width, 128), F32),
            *exchange,
            *exchange,
            *Sum.scratch(conv_rows, n, nx),
            *Sum.scratch(down_rows, n, nx),
            pltpu.SemaphoreType.DMA((copies,)),
            pltpu.SemaphoreType.DMA((copies,)),
            pltpu.SemaphoreType.DMA((2,)),
        ],
        compiler_params=pltpu.CompilerParams(
            collective_id=0, has_side_effects=True, vmem_limit_bytes=48 << 20
        ),
    )(*args)
    grad_conv = conv[:, :, :conv_rows].astype(F32).reshape(offsets, width, width)
    grad_down = jnp.concatenate([down[0], down[1]], -1).astype(F32).reshape(OCT * width, 256)
    return (coarse, grad_conv, grad_down)


def solution(mesh):
    n, nx = math.isqrt(mesh.shape["blk"] // 2), mesh.shape["dp"]
    in_specs = (
        P("dp", "blk", None),
        P("dp", None, "blk"),
        P("dp", None),
        P("dp", "blk"),
        P("dp", "blk"),
        P(),
        P(),
        P("dp", "blk", None),
    )
    out_specs = (P("dp", "blk", None), P(), P())
    return jax.shard_map(
        functools.partial(body, n, nx),
        mesh=mesh,
        in_specs=in_specs,
        out_specs=out_specs,
        check_vma=False,
    )
```

```python
import functools
import math

import jax
import jax.numpy as jnp
from jax import lax
from jax.experimental import pallas as pl
from jax.experimental.pallas import tpu as pltpu
from jax.sharding import PartitionSpec as P

OCT = 8
HALO = 64
F32 = jnp.float32
BF16 = jnp.bfloat16
MESH = pl.DeviceIdType.MESH


def iota(shape, dim):
    return lax.broadcasted_iota(jnp.int32, shape, dim)


def dot(a, b, ca, cb):
    return lax.dot_general(a, b, (((ca,), (cb,)), ((), ())), preferred_element_type=F32)


def up16(rows):
    return -(-rows // 16) * 16


class Place:
    def __init__(self, n, nx):
        blk = lax.axis_index("blk")
        self.n, self.nx = n, nx
        self.blk, self.x = blk, lax.axis_index("dp")
        self.c = lax.rem(blk, 2)
        chip = lax.div(blk, 2)
        z, y = lax.div(chip, n), lax.rem(chip, n)
        self.a = (1 - self.c) * y + self.c * z
        self.b = (1 - self.c) * z + self.c * y

    def of(self, a, b):
        c, n = self.c, self.n
        return ((1 - c) * (b * n + a) + c * (a * n + b)) * 2 + c

    def axis(self, name):
        if name == "x":
            return self.nx, self.x, self.along_x
        return (self.n, self.a, self.along_a) if name == "a" else (self.n, self.b, self.along_b)

    def along_a(self, p):
        return (self.of(lax.rem(self.a + p, self.n), self.b), self.x)

    def along_b(self, p):
        return (self.of(self.a, lax.rem(self.b + p, self.n)), self.x)

    def along_x(self, p):
        return (self.blk, lax.rem(self.x + p, self.nx))

    def other_core(self):
        return (self.blk + 1 - 2 * self.c, self.x)

    def next_block(self, p, count):
        return (lax.rem(self.blk + p, count), self.x)


class Sender:
    def __init__(self, send_sem, recv_sem):
        self.send_sem, self.recv_sem, self.used, self.all = send_sem, recv_sem, 0, []

    def start(self, src, dst, device):
        copy = pltpu.make_async_remote_copy(
            src_ref=src,
            dst_ref=dst,
            send_sem=self.send_sem.at[self.used],
            recv_sem=self.recv_sem.at[self.used],
            device_id=device,
            device_id_type=MESH,
        )
        self.used += 1
        copy.start()
        self.all.append(copy)
        return copy

    def finish(self):
        for copy in self.all:
            copy.wait_send()


def arrived(copies):
    for copy in copies:
        copy.wait_recv()


class Exchange:
    def __init__(self, place, sender, bufs):
        self.place, self.sender = place, sender
        self.send1, self.recv1, self.send2, self.recv2, self.got = bufs

    def start(self, rows):
        pc, n = self.place, self.place.n
        self.send1[...] = rows.reshape(self.send1.shape)
        self.copies = [
            self.sender.start(
                self.send1.at[lax.rem(pc.a + p, n)], self.recv1.at[pc.a], pc.along_a(p)
            )
            for p in range(1, n)
        ]
        self.recv1[pc.a] = self.send1[pc.a]

    def second(self, swap):
        pc, n = self.place, self.place.n
        arrived(self.copies)
        flat = self.recv1[...].reshape(swap.shape[1], -1)
        moved = jnp.dot(swap[...], flat, preferred_element_type=F32).astype(BF16)
        self.send2[...] = moved.reshape(self.send2.shape)
        self.copies = [
            self.sender.start(
                self.send2.at[lax.rem(pc.b + p, n)], self.recv2.at[pc.b], pc.along_b(p)
            )
            for p in range(1, n)
        ]
        self.recv2[pc.b] = self.send2[pc.b]

    def third(self):
        pc = self.place
        arrived(self.copies)
        self.copies = [
            self.sender.start(self.recv2.at[:, 1 - pc.c], self.got.at[pc.c], pc.other_core())
        ]
        self.got[pc.c] = self.recv2[:, pc.c]

    def result(self):
        arrived(self.copies)
        flat = self.got[...]
        return flat.reshape(-1, flat.shape[-1])


class Sum:
    def __init__(self, place, sender, rows, order, bufs, out):
        self.place, self.sender, self.out = place, sender, out
        self.axes = [place.axis(name) for name in order]
        self.rows, self.part, self.wide = self.sizes(rows, *[axis[0] for axis in self.axes[:2]])
        self.s0, self.r0, self.own, self.s1, self.r1 = bufs[:5]
        self.s2, self.r2, self.s3, self.g2, self.g1 = bufs[5:]

    @staticmethod
    def sizes(rows, n1, n2):
        chunk = rows // n1
        return chunk, up16(-(-chunk // n2)), up16(chunk)

    @staticmethod
    def scratch(rows, n1, n2, n3):
        _, part, wide = Sum.sizes(rows, n1, n2)
        return [
            pltpu.VMEM((rows, 128), BF16),
            pltpu.VMEM((rows, 128), BF16),
            pltpu.VMEM((rows, 128), F32),
            pltpu.VMEM((n1, wide, 128), BF16),
            pltpu.VMEM((n1, wide, 128), BF16),
            pltpu.VMEM((n2, part, 128), F32),
            pltpu.VMEM((n2, part, 128), F32),
            pltpu.VMEM((n3, part, 128), F32),
            pltpu.VMEM((n2 * part, 128), BF16),
            pltpu.VMEM((n1, wide, 128), BF16),
        ]

    def start(self, theirs, mine):
        self.s0[...] = theirs().astype(BF16)
        self.copies = [self.sender.start(self.s0, self.r0, self.place.other_core())]
        self.own[...] = mine()

    def first(self):
        (n, me, along), rows = self.axes[0], self.rows
        arrived(self.copies)
        for q in range(n):
            chunk = pl.ds(q * rows, rows)
            total = self.own[chunk] + self.r0[chunk].astype(F32)
            self.own[chunk] = total
            self.s1[q, pl.ds(0, rows)] = total.astype(BF16)
            if self.wide > rows:
                self.s1[q, pl.ds(rows, self.wide - rows)] = jnp.zeros(
                    (self.wide - rows, 128), BF16
                )
        self.copies = [
            self.sender.start(self.s1.at[lax.rem(me + p, n)], self.r1.at[p], along(p))
            for p in range(1, n)
        ]

    def second(self):
        (n1, me1, _), (n, me, along), rows = self.axes[0], self.axes[1], self.rows
        arrived(self.copies)
        total = self.own[pl.ds(pl.multiple_of(me1 * rows, 8), rows)]
        for p in range(1, n1):
            total += self.r1[p][:rows].astype(F32)
        spare = n * self.part - rows
        if spare:
            total = jnp.concatenate([total, jnp.zeros((spare, 128), F32)], 0)
        self.s2[...] = total.reshape(self.s2.shape)
        self.copies = [
            self.sender.start(self.s2.at[lax.rem(me + p, n)], self.r2.at[p], along(p))
            for p in range(1, n)
        ]

    def third(self):
        (n2, me2, _), (n, me, along) = self.axes[1:]
        arrived(self.copies)
        total = self.s2[me2]
        for p in range(1, n2):
            total += self.r2[p]
        self.s3[me] = total
        self.copies = [
            self.sender.start(self.s3.at[me], self.s3.at[me], along(p)) for p in range(1, n)
        ]

    def back_second(self):
        n, me, along = self.axes[1]
        arrived(self.copies)
        total = self.s3[0]
        for x in range(1, self.axes[2][0]):
            total += self.s3[x]
        mine = pl.ds(pl.multiple_of(me * self.part, 16), self.part)
        self.g2[mine] = total.astype(BF16)
        self.copies = [
            self.sender.start(self.g2.at[mine], self.g2.at[mine], along(p)) for p in range(1, n)
        ]

    def back_first(self):
        n, me, along = self.axes[0]
        arrived(self.copies)
        self.g1[me] = self.g2[pl.ds(0, self.wide)]
        self.copies = [
            self.sender.start(self.g1.at[me], self.g1.at[me], along(p)) for p in range(1, n)
        ]

    def back_core(self, sem):
        pc = self.place
        arrived(self.copies)
        self.copies = [self.sender.start(self.g1, self.out.at[pc.c], pc.other_core())]
        self.kept = pltpu.make_async_copy(self.g1, self.out.at[pc.c], sem)
        self.kept.start()

    def result(self):
        arrived(self.copies)
        self.kept.wait()


def conv_split(rows):
    return rows * 13 // 27


ORDERS = (("a", "b", "x"), ("x", "a", "b"), ("x", "a", "b"))


def kernel(n, nx, cap, *refs):
    given, (out_coarse, *outs), refs = refs[:8], refs[8:12], refs[12:]
    (
        kernel_map,
        block_counts,
        send_position,
        cell_source,
        conv_weight,
        down_weight,
        cotangent,
        raw,
        weight_t,
        picked,
        by_child,
        send_hot,
        swap,
        down_grad,
        coarse,
        *rest,
    ) = refs
    *rest, send_sem, recv_sem, local_sem, load_sem = rest
    count = 2 * n * n
    features = given[0]
    offsets = conv_weight.shape[0]
    rows, width = features.shape[1], features.shape[2]
    cells = count * cap
    half = offsets * width // 2
    pc = Place(n, nx)
    sender = Sender(send_sem, recv_sem)

    barrier = pltpu.get_barrier_semaphore()
    partners = [pc.along_a(p) for p in range(1, n)] + [pc.along_b(p) for p in range(1, n)]
    partners += [pc.along_x(p) for p in range(1, nx)]
    partners += [pc.other_core(), pc.next_block(1, count), pc.next_block(count - 1, count)]
    for device in partners:
        pl.semaphore_signal(barrier, inc=1, device_id=device, device_id_type=MESH)

    targets = [raw.at[pl.ds(HALO, rows)], *refs[:7]]
    sources = [features.at[0], *given[1:]]
    loads = [
        pltpu.make_async_copy(src, dst, load_sem.at[i])
        for i, (src, dst) in enumerate(zip(sources, targets))
    ]
    for i in (7, 6, 4, 0, 2, 3, 1, 5):
        loads[i].start()
    pl.semaphore_wait(barrier, len(partners))

    halo = [
        sender.start(
            features.at[0, pl.ds(rows - HALO, HALO)],
            raw.at[pl.ds(0, HALO)],
            pc.next_block(1, count),
        ),
        sender.start(
            features.at[0, pl.ds(0, HALO)],
            raw.at[pl.ds(HALO + rows, HALO)],
            pc.next_block(count - 1, count),
        ),
    ]

    forward = Exchange(pc, sender, rest[0:5])
    backward = Exchange(pc, sender, rest[5:10])
    first_rows = conv_split(half)
    sums = [
        Sum(pc, sender, total, order, rest[10 + 10 * i : 20 + 10 * i], outs[i])
        for i, (total, order) in enumerate(
            zip((first_rows, half - first_rows, OCT * width), ORDERS)
        )
    ]
    sum_conv, sum_down = sums[:2], sums[2]

    r = iota((cells, 1), 0)
    slot, r1 = lax.rem(r, cap), lax.div(r, cap)
    to_b, r2 = lax.rem(r1, n), lax.div(r1, n)
    to_c, to_a = lax.rem(r2, 2), lax.div(r2, 2)
    chip = jnp.where(pc.c == 0, to_b * n + to_a, to_a * n + to_b)
    goes_to = (chip * 2 + to_c) * cap + slot
    from_a, from_b, from_c = to_b, lax.rem(r2, n), lax.div(r2, n)
    chip = jnp.where(from_c == 0, from_b * n + from_a, from_a * n + from_b)
    comes_from = (chip * 2 + from_c) * cap + slot

    def hot(at, values):
        return jnp.where(at == values, 1.0, 0.0).astype(BF16)

    for i in (7, 6, 4):
        loads[i].wait()
    for j in range(OCT):
        part = dot(cotangent[0], down_weight[pl.ds(j * width, width)], 1, 1)
        by_child[pl.ds(j, rows // 4, stride=OCT)] = part.astype(BF16).astype(F32)
    children = cell_source[...]
    backward.start(
        jnp.dot(hot(goes_to, children), by_child[...].astype(BF16), preferred_element_type=F32)
        .astype(BF16)
    )

    loads[0].wait()
    loads[2].wait()

    def live_of(block, inside):
        counted = block_counts[0, lax.rem(block, count)]
        front = lax.div(counted, 2)
        return (inside < front) | (inside >= rows - (counted - front))

    loads[5].wait()
    for k in range(offsets):
        weight_t[:, pl.ds(k * width, width)] = conv_weight[k].astype(F32).T.astype(BF16)
    loads[1].wait()
    lane = lax.rem(iota((1, rows), 1), 128)
    window = iota((2 * HALO + 128, 128), 0)
    live_t = live_of(pc.blk, iota((1, rows), 1))
    live = jnp.concatenate(
        [
            live_of(pc.blk + count - 1, iota((HALO, width), 0) + rows - HALO),
            live_of(pc.blk, iota((rows, width), 0)),
            live_of(pc.blk + 1, iota((HALO, width), 0)),
        ],
        0,
    )

    arrived(halo)
    table_t = jnp.where(live, raw[...].astype(F32), 0.0).T.astype(BF16)
    for k in range(offsets):
        entry = kernel_map[k]
        index = jnp.where(entry >= 0, entry + lane, -1)
        for t in range(rows // 128):
            chosen = hot(window, index[:, t * 128 : (t + 1) * 128])
            got = jnp.dot(
                table_t[:, t * 128 : t * 128 + 128 + 2 * HALO], chosen, preferred_element_type=F32
            )
            picked[pl.ds(k * width, width), pl.ds(t * 128, 128)] = got.astype(BF16)

    loads[3].wait()
    position = send_position[...]
    send_hot[...] = hot(goes_to, position)
    pre = jnp.dot(weight_t[...], picked[...], preferred_element_type=F32)
    sig = 1.0 / (1.0 + jnp.exp(-pre))
    hidden = jnp.where(live_t, pre * sig, 0.0).astype(BF16)
    forward.start(dot(send_hot[...], hidden, 1, 1).astype(BF16))

    swapped = ((to_b * 2 + to_c) * n + to_a) * cap + slot
    swap[...] = hot(swapped, iota((1, cells), 1))
    backward.second(swap)
    from_owner = hot(comes_from, position)
    slope = jnp.where(live_t, sig * (1.0 + pre * (1.0 - sig)), 0.0)
    forward.second(swap)
    backward.third()
    grad_hidden = dot(backward.result(), from_owner, 0, 0)
    grad_pre = (grad_hidden * slope).astype(BF16)

    def conv_rows(h, start, size):
        chosen = picked[pl.ds(pl.multiple_of(h * half + start, 16), size)]
        return dot(chosen, grad_pre, 1, 1)

    for job, start, size in (
        (sum_conv[0], 0, first_rows),
        (sum_conv[1], first_rows, half - first_rows),
    ):
        job.start(
            functools.partial(conv_rows, 1 - pc.c, start, size),
            functools.partial(conv_rows, pc.c, start, size),
        )
    for job in sum_conv:
        job.first()
    forward.third()

    to_child = hot(comes_from, children)
    by_child[...] = dot(to_child, forward.result(), 0, 0)
    total = jnp.zeros(coarse.shape[1:], F32)
    for j in range(OCT):
        child = by_child[pl.ds(j, rows // 4, stride=OCT)].astype(BF16)
        grad = dot(child, cotangent[0], 0, 0)
        for h in range(2):
            down_grad[h, pl.ds(j * width, width)] = grad[:, h * 128 : (h + 1) * 128]
        total += jnp.dot(
            child, down_weight[pl.ds(j * width, width)], preferred_element_type=F32
        )
    sum_down.start(lambda: down_grad[1 - pc.c], lambda: down_grad[pc.c])
    coarse[0] = total.astype(BF16)
    kept = pltpu.make_async_copy(coarse, out_coarse, local_sem.at[3])
    kept.start()

    sum_down.first()
    for job in sums:
        job.second()
    for job in sums:
        job.third()
    for job in sums:
        job.back_second()
    for job in sums:
        job.back_first()
    for i, job in enumerate(sums):
        job.back_core(local_sem.at[i])
    for job in sums:
        job.result()
    kept.wait()
    sender.finish()


def finish(conv_a, conv_x, down, out_conv, out_down, *refs):
    *stored, full_conv, full_down, load_sem, save_sem = refs
    given = (conv_a, conv_x, down)
    half = out_conv.shape[0] // 2
    first_rows = conv_split(half)
    loads = [
        [pltpu.make_async_copy(src.at[h], dst.at[h], load_sem.at[i, h]) for h in range(2)]
        for i, (src, dst) in enumerate(zip(given, stored))
    ]
    for i in range(3):
        for h in range(2):
            loads[i][h].start()
    saves = []
    for i, start, rows in ((0, 0, first_rows), (1, first_rows, half - first_rows)):
        for h in range(2):
            loads[i][h].wait()
            n = stored[i].shape[1]
            chunk = rows // n
            for q in range(n):
                full_conv[pl.ds(h * half + start + q * chunk, chunk)] = stored[i][
                    h, q, pl.ds(0, chunk)
                ].astype(F32)
            at = pl.ds(h * half + start, rows)
            saves.append(
                pltpu.make_async_copy(full_conv.at[at], out_conv.at[at], save_sem.at[i, h])
            )
            saves[-1].start()
    for h in range(2):
        loads[2][h].wait()
        full_down[:, pl.ds(h * 128, 128)] = (
            stored[2][h].reshape(full_down.shape[0], 128).astype(F32)
        )
    saves.append(pltpu.make_async_copy(full_down, out_down, save_sem.at[2, 0]))
    saves[-1].start()
    for save in saves:
        save.wait()


def body(n, nx, *args):
    args = list(args)
    args[1] = jnp.transpose(args[1], (1, 0, 2))
    features, _, _, _, cell_source, conv_weight, _, cotangent = args
    rows, width = features.shape[1:]
    offsets = conv_weight.shape[0]
    cells = cell_source.shape[1]
    cap = cells // (2 * n * n)
    half = offsets * width // 2
    first_rows = conv_split(half)
    exchange = [
        pltpu.VMEM((n, cells // n, width), BF16),
        pltpu.VMEM((n, cells // n, width), BF16),
        pltpu.VMEM((n, 2, cells // n // 2, width), BF16),
        pltpu.VMEM((n, 2, cells // n // 2, width), BF16),
        pltpu.VMEM((2, n, cells // n // 2, width), BF16),
    ]
    sizes = {"a": n, "b": n, "x": nx}
    jobs = [
        (total, *[sizes[name] for name in order])
        for total, order in zip((first_rows, half - first_rows, OCT * width), ORDERS)
    ]
    copies = 2 + 2 * (2 * (n - 1) + 1)
    copies += sum(2 + 2 * (n1 - 1) + 2 * (n2 - 1) + n3 - 1 for _, n1, n2, n3 in jobs)
    hbm = pl.BlockSpec(memory_space=pl.ANY)
    coarse, *parts = pl.pallas_call(
        functools.partial(kernel, n, nx, cap),
        out_shape=[jax.ShapeDtypeStruct(cotangent.shape, BF16)]
        + [
            jax.ShapeDtypeStruct((2, n1, up16(total // n1), 128), BF16) for total, n1, _, _ in jobs
        ],
        in_specs=[hbm] * 8,
        out_specs=[hbm] * 4,
        scratch_shapes=[
            *[
                (pltpu.SMEM if i == 2 else pltpu.VMEM)(arg.shape, arg.dtype)
                for i, arg in enumerate(args)
                if i > 0
            ],
            pltpu.VMEM((rows + 2 * HALO, width), BF16),
            pltpu.VMEM((width, offsets * width), BF16),
            pltpu.VMEM((offsets * width, rows), BF16),
            pltpu.VMEM((cells, width), F32),
            pltpu.VMEM((cells, rows), BF16),
            pltpu.VMEM((cells, cells), BF16),
            pltpu.VMEM((2, OCT * width, 128), F32),
            pltpu.VMEM(cotangent.shape, BF16),
            *exchange,
            *exchange,
            *[ref for job in jobs for ref in Sum.scratch(*job)],
            pltpu.SemaphoreType.DMA((copies,)),
            pltpu.SemaphoreType.DMA((copies,)),
            pltpu.SemaphoreType.DMA((4,)),
            pltpu.SemaphoreType.DMA((8,)),
        ],
        compiler_params=pltpu.CompilerParams(
            collective_id=0, has_side_effects=True, vmem_limit_bytes=64 << 20
        ),
    )(*args)
    grad_conv, grad_down = pl.pallas_call(
        finish,
        out_shape=[
            jax.ShapeDtypeStruct((offsets * width, width), F32),
            jax.ShapeDtypeStruct((OCT * width, 256), F32),
        ],
        in_specs=[hbm] * 3,
        out_specs=[hbm] * 2,
        scratch_shapes=[
            *[pltpu.VMEM(part.shape, BF16) for part in parts],
            pltpu.VMEM((offsets * width, width), F32),
            pltpu.VMEM((OCT * width, 256), F32),
            pltpu.SemaphoreType.DMA((3, 2)),
            pltpu.SemaphoreType.DMA((3, 2)),
        ],
        compiler_params=pltpu.CompilerParams(vmem_limit_bytes=64 << 20),
    )(*parts)
    return (coarse, grad_conv.reshape(offsets, width, width), grad_down)


def solution(mesh):
    n, nx = math.isqrt(mesh.shape["blk"] // 2), mesh.shape["dp"]
    in_specs = (
        P("dp", "blk", None),
        P("dp", None, "blk"),
        P("dp", None),
        P("dp", "blk"),
        P("dp", "blk"),
        P(),
        P(),
        P("dp", "blk", None),
    )
    out_specs = (P("dp", "blk", None), P(), P())
    return jax.shard_map(
        functools.partial(body, n, nx),
        mesh=mesh,
        in_specs=in_specs,
        out_specs=out_specs,
        check_vma=False,
    )
```

```python
import functools
import math

import jax
import jax.numpy as jnp
from jax import lax
from jax.experimental import pallas as pl
from jax.experimental.pallas import tpu as pltpu
from jax.sharding import PartitionSpec as P

OCT = 8
HALO = 64
F32 = jnp.float32
BF16 = jnp.bfloat16
MESH = pl.DeviceIdType.MESH


def iota(shape, dim):
    return lax.broadcasted_iota(jnp.int32, shape, dim)


def dot(a, b, ca, cb):
    return lax.dot_general(a, b, (((ca,), (cb,)), ((), ())), preferred_element_type=F32)


def up16(rows):
    return -(-rows // 16) * 16


class Place:
    def __init__(self, n, nx):
        blk = lax.axis_index("blk")
        self.n, self.nx = n, nx
        self.blk, self.x = blk, lax.axis_index("dp")
        self.c = lax.rem(blk, 2)
        chip = lax.div(blk, 2)
        z, y = lax.div(chip, n), lax.rem(chip, n)
        self.a = (1 - self.c) * y + self.c * z
        self.b = (1 - self.c) * z + self.c * y

    def of(self, a, b):
        c, n = self.c, self.n
        return ((1 - c) * (b * n + a) + c * (a * n + b)) * 2 + c

    def axis(self, name):
        if name == "x":
            return self.nx, self.x, self.along_x
        return (self.n, self.a, self.along_a) if name == "a" else (self.n, self.b, self.along_b)

    def along_a(self, p):
        return (self.of(lax.rem(self.a + p, self.n), self.b), self.x)

    def along_b(self, p):
        return (self.of(self.a, lax.rem(self.b + p, self.n)), self.x)

    def along_x(self, p):
        return (self.blk, lax.rem(self.x + p, self.nx))

    def other_core(self):
        return (self.blk + 1 - 2 * self.c, self.x)

    def next_block(self, p, count):
        return (lax.rem(self.blk + p, count), self.x)


class Sender:
    def __init__(self, send_sem, recv_sem):
        self.send_sem, self.recv_sem, self.used, self.all = send_sem, recv_sem, 0, []

    def start(self, src, dst, device):
        copy = pltpu.make_async_remote_copy(
            src_ref=src,
            dst_ref=dst,
            send_sem=self.send_sem.at[self.used],
            recv_sem=self.recv_sem.at[self.used],
            device_id=device,
            device_id_type=MESH,
        )
        self.used += 1
        copy.start()
        self.all.append(copy)
        return copy

    def finish(self):
        for copy in self.all:
            copy.wait_send()


def arrived(copies):
    for copy in copies:
        copy.wait_recv()


class Exchange:
    def __init__(self, place, sender, bufs):
        self.place, self.sender = place, sender
        self.send1, self.recv1, self.send2, self.recv2, self.got = bufs

    def start(self, rows):
        pc, n = self.place, self.place.n
        self.send1[...] = rows.reshape(self.send1.shape)
        self.copies = [
            self.sender.start(
                self.send1.at[lax.rem(pc.a + p, n)], self.recv1.at[pc.a], pc.along_a(p)
            )
            for p in range(1, n)
        ]
        self.recv1[pc.a] = self.send1[pc.a]

    def second(self, swap):
        pc, n = self.place, self.place.n
        arrived(self.copies)
        flat = self.recv1[...].reshape(swap.shape[1], -1)
        moved = jnp.dot(swap[...], flat, preferred_element_type=F32).astype(BF16)
        self.send2[...] = moved.reshape(self.send2.shape)
        self.copies = [
            self.sender.start(
                self.send2.at[lax.rem(pc.b + p, n)], self.recv2.at[pc.b], pc.along_b(p)
            )
            for p in range(1, n)
        ]
        self.recv2[pc.b] = self.send2[pc.b]

    def third(self):
        pc = self.place
        arrived(self.copies)
        self.copies = [
            self.sender.start(self.recv2.at[:, 1 - pc.c], self.got.at[pc.c], pc.other_core())
        ]
        self.got[pc.c] = self.recv2[:, pc.c]

    def result(self):
        arrived(self.copies)
        flat = self.got[...]
        return flat.reshape(-1, flat.shape[-1])


class Sum:
    def __init__(self, place, sender, rows, order, bufs, out):
        self.place, self.sender, self.out = place, sender, out
        self.axes = [place.axis(name) for name in order]
        self.rows, self.part, self.wide = self.sizes(rows, *[axis[0] for axis in self.axes[:2]])
        self.s0, self.r0, self.own, self.s1, self.r1 = bufs[:5]
        self.s2, self.r2, self.s3, self.g2, self.g1 = bufs[5:]

    @staticmethod
    def sizes(rows, n1, n2):
        chunk = rows // n1
        return chunk, up16(-(-chunk // n2)), up16(chunk)

    @staticmethod
    def scratch(rows, n1, n2, n3, middle):
        _, part, wide = Sum.sizes(rows, n1, n2)
        return [
            pltpu.VMEM((rows, 128), BF16),
            pltpu.VMEM((rows, 128), BF16),
            pltpu.VMEM((rows, 128), F32),
            pltpu.VMEM((n1, wide, 128), BF16),
            pltpu.VMEM((n1, wide, 128), BF16),
            pltpu.VMEM((n2, part, 128), middle),
            pltpu.VMEM((n2, part, 128), middle),
            pltpu.VMEM((n3, part, 128), middle),
            pltpu.VMEM((n2 * part, 128), BF16),
            pltpu.VMEM((n1, wide, 128), BF16),
        ]

    def start(self, theirs, mine):
        self.s0[...] = theirs().astype(BF16)
        self.copies = [self.sender.start(self.s0, self.r0, self.place.other_core())]
        self.own[...] = mine()

    def first(self):
        (n, me, along), rows = self.axes[0], self.rows
        arrived(self.copies)
        for q in range(n):
            chunk = pl.ds(q * rows, rows)
            total = self.own[chunk] + self.r0[chunk].astype(F32)
            self.own[chunk] = total
            self.s1[q, pl.ds(0, rows)] = total.astype(BF16)
            if self.wide > rows:
                self.s1[q, pl.ds(rows, self.wide - rows)] = jnp.zeros(
                    (self.wide - rows, 128), BF16
                )
        self.copies = [
            self.sender.start(self.s1.at[lax.rem(me + p, n)], self.r1.at[p], along(p))
            for p in range(1, n)
        ]

    def second(self):
        (n1, me1, _), (n, me, along), rows = self.axes[0], self.axes[1], self.rows
        arrived(self.copies)
        total = self.own[pl.ds(pl.multiple_of(me1 * rows, 8), rows)]
        for p in range(1, n1):
            total += self.r1[p][:rows].astype(F32)
        spare = n * self.part - rows
        if spare:
            total = jnp.concatenate([total, jnp.zeros((spare, 128), F32)], 0)
        self.s2[...] = total.reshape(self.s2.shape).astype(self.s2.dtype)
        self.copies = [
            self.sender.start(self.s2.at[lax.rem(me + p, n)], self.r2.at[p], along(p))
            for p in range(1, n)
        ]

    def third(self):
        (n2, me2, _), (n, me, along) = self.axes[1:]
        arrived(self.copies)
        total = self.s2[me2].astype(F32)
        for p in range(1, n2):
            total += self.r2[p].astype(F32)
        self.s3[me] = total.astype(self.s3.dtype)
        self.copies = [
            self.sender.start(self.s3.at[me], self.s3.at[me], along(p)) for p in range(1, n)
        ]

    def back_second(self):
        n, me, along = self.axes[1]
        arrived(self.copies)
        total = self.s3[0].astype(F32)
        for x in range(1, self.axes[2][0]):
            total += self.s3[x].astype(F32)
        mine = pl.ds(pl.multiple_of(me * self.part, 16), self.part)
        self.g2[mine] = total.astype(BF16)
        self.copies = [
            self.sender.start(self.g2.at[mine], self.g2.at[mine], along(p)) for p in range(1, n)
        ]

    def back_first(self):
        n, me, along = self.axes[0]
        arrived(self.copies)
        self.g1[me] = self.g2[pl.ds(0, self.wide)]
        self.copies = [
            self.sender.start(self.g1.at[me], self.g1.at[me], along(p)) for p in range(1, n)
        ]

    def back_core(self, sem):
        pc = self.place
        arrived(self.copies)
        self.copies = [self.sender.start(self.g1, self.out.at[pc.c], pc.other_core())]
        self.kept = pltpu.make_async_copy(self.g1, self.out.at[pc.c], sem)
        self.kept.start()

    def result(self):
        arrived(self.copies)
        self.kept.wait()


def conv_split(rows):
    return rows * 13 // 27


ORDERS = (("a", "b", "x"), ("x", "a", "b"), ("x", "a", "b"))


def kernel(n, nx, cap, *refs):
    given, (out_coarse, *outs), refs = refs[:8], refs[8:12], refs[12:]
    (
        kernel_map,
        block_counts,
        send_position,
        cell_source,
        conv_weight,
        down_weight,
        cotangent,
        raw,
        weight_t,
        picked,
        by_child,
        send_hot,
        swap,
        down_grad,
        coarse,
        *rest,
    ) = refs
    *rest, send_sem, recv_sem, local_sem, load_sem = rest
    count = 2 * n * n
    features = given[0]
    offsets = conv_weight.shape[0]
    rows, width = features.shape[1], features.shape[2]
    cells = count * cap
    half = offsets * width // 2
    pc = Place(n, nx)
    sender = Sender(send_sem, recv_sem)

    barrier = pltpu.get_barrier_semaphore()
    partners = [pc.along_a(p) for p in range(1, n)] + [pc.along_b(p) for p in range(1, n)]
    partners += [pc.along_x(p) for p in range(1, nx)]
    partners += [pc.other_core(), pc.next_block(1, count), pc.next_block(count - 1, count)]
    for device in partners:
        pl.semaphore_signal(barrier, inc=1, device_id=device, device_id_type=MESH)

    targets = [raw.at[pl.ds(HALO, rows)], *refs[:7]]
    sources = [features.at[0], *given[1:]]
    loads = [
        pltpu.make_async_copy(src, dst, load_sem.at[i])
        for i, (src, dst) in enumerate(zip(sources, targets))
    ]
    for i in (7, 6, 4, 0, 2, 3, 1, 5):
        loads[i].start()
    pl.semaphore_wait(barrier, len(partners))

    halo = [
        sender.start(
            features.at[0, pl.ds(rows - HALO, HALO)],
            raw.at[pl.ds(0, HALO)],
            pc.next_block(1, count),
        ),
        sender.start(
            features.at[0, pl.ds(0, HALO)],
            raw.at[pl.ds(HALO + rows, HALO)],
            pc.next_block(count - 1, count),
        ),
    ]

    forward = Exchange(pc, sender, rest[0:5])
    backward = Exchange(pc, sender, rest[5:10])
    first_rows = conv_split(half)
    sums = [
        Sum(pc, sender, total, order, rest[10 + 10 * i : 20 + 10 * i], outs[i])
        for i, (total, order) in enumerate(
            zip((first_rows, half - first_rows, OCT * width), ORDERS)
        )
    ]
    sum_conv, sum_down = sums[:2], sums[2]

    r = iota((cells, 1), 0)
    slot, r1 = lax.rem(r, cap), lax.div(r, cap)
    to_b, r2 = lax.rem(r1, n), lax.div(r1, n)
    to_c, to_a = lax.rem(r2, 2), lax.div(r2, 2)
    chip = jnp.where(pc.c == 0, to_b * n + to_a, to_a * n + to_b)
    goes_to = (chip * 2 + to_c) * cap + slot
    from_a, from_b, from_c = to_b, lax.rem(r2, n), lax.div(r2, n)
    chip = jnp.where(from_c == 0, from_b * n + from_a, from_a * n + from_b)
    comes_from = (chip * 2 + from_c) * cap + slot

    def hot(at, values):
        return jnp.where(at == values, 1.0, 0.0).astype(BF16)

    for i in (7, 6, 4):
        loads[i].wait()
    for j in range(OCT):
        part = dot(cotangent[0], down_weight[pl.ds(j * width, width)], 1, 1)
        by_child[pl.ds(j, rows // 4, stride=OCT)] = part.astype(BF16).astype(F32)
    children = cell_source[...]
    backward.start(
        jnp.dot(hot(goes_to, children), by_child[...].astype(BF16), preferred_element_type=F32)
        .astype(BF16)
    )

    loads[0].wait()
    loads[2].wait()

    def live_of(block, inside):
        counted = block_counts[0, lax.rem(block, count)]
        front = lax.div(counted, 2)
        return (inside < front) | (inside >= rows - (counted - front))

    loads[5].wait()
    for k in range(offsets):
        weight_t[:, pl.ds(k * width, width)] = conv_weight[k].astype(F32).T.astype(BF16)
    loads[1].wait()
    lane = lax.rem(iota((1, rows), 1), 128)
    window = iota((2 * HALO + 128, 128), 0)
    live_t = live_of(pc.blk, iota((1, rows), 1))
    live = jnp.concatenate(
        [
            live_of(pc.blk + count - 1, iota((HALO, width), 0) + rows - HALO),
            live_of(pc.blk, iota((rows, width), 0)),
            live_of(pc.blk + 1, iota((HALO, width), 0)),
        ],
        0,
    )

    arrived(halo)
    table_t = jnp.where(live, raw[...].astype(F32), 0.0).T.astype(BF16)
    for k in range(offsets):
        entry = kernel_map[k]
        index = jnp.where(entry >= 0, entry + lane, -1)
        for t in range(rows // 128):
            chosen = hot(window, index[:, t * 128 : (t + 1) * 128])
            got = jnp.dot(
                table_t[:, t * 128 : t * 128 + 128 + 2 * HALO], chosen, preferred_element_type=F32
            )
            picked[pl.ds(k * width, width), pl.ds(t * 128, 128)] = got.astype(BF16)

    loads[3].wait()
    position = send_position[...]
    send_hot[...] = hot(goes_to, position)
    pre = jnp.dot(weight_t[...], picked[...], preferred_element_type=F32)
    sig = 1.0 / (1.0 + jnp.exp(-pre))
    hidden = jnp.where(live_t, pre * sig, 0.0).astype(BF16)
    forward.start(dot(send_hot[...], hidden, 1, 1).astype(BF16))

    swapped = ((to_b * 2 + to_c) * n + to_a) * cap + slot
    swap[...] = hot(swapped, iota((1, cells), 1))
    backward.second(swap)
    from_owner = hot(comes_from, position)
    slope = jnp.where(live_t, sig * (1.0 + pre * (1.0 - sig)), 0.0)
    forward.second(swap)
    backward.third()
    grad_hidden = dot(backward.result(), from_owner, 0, 0)
    grad_pre = (grad_hidden * slope).astype(BF16)

    def conv_rows(h, start, size):
        chosen = picked[pl.ds(pl.multiple_of(h * half + start, 16), size)]
        return dot(chosen, grad_pre, 1, 1)

    for job, start, size in (
        (sum_conv[0], 0, first_rows),
        (sum_conv[1], first_rows, half - first_rows),
    ):
        job.start(
            functools.partial(conv_rows, 1 - pc.c, start, size),
            functools.partial(conv_rows, pc.c, start, size),
        )
    for job in sum_conv:
        job.first()
    forward.third()

    to_child = hot(comes_from, children)
    by_child[...] = dot(to_child, forward.result(), 0, 0)
    total = jnp.zeros(coarse.shape[1:], F32)
    for j in range(OCT):
        child = by_child[pl.ds(j, rows // 4, stride=OCT)].astype(BF16)
        grad = dot(child, cotangent[0], 0, 0)
        for h in range(2):
            down_grad[h, pl.ds(j * width, width)] = grad[:, h * 128 : (h + 1) * 128]
        total += jnp.dot(
            child, down_weight[pl.ds(j * width, width)], preferred_element_type=F32
        )
    sum_down.start(lambda: down_grad[1 - pc.c], lambda: down_grad[pc.c])
    coarse[0] = total.astype(BF16)
    kept = pltpu.make_async_copy(coarse, out_coarse, local_sem.at[3])
    kept.start()

    sum_down.first()
    for job in sums:
        job.second()
    for job in sums:
        job.third()
    for job in sums:
        job.back_second()
    for job in sums:
        job.back_first()
    for i, job in enumerate(sums):
        job.back_core(local_sem.at[i])
    for job in sums:
        job.result()
    kept.wait()
    sender.finish()


def finish(coarse, conv_a, conv_x, down, out_coarse, out_conv, out_down, *refs):
    *stored, full_conv, full_down, load_sem, save_sem = refs
    given = (conv_a, conv_x, down)
    half = out_conv.shape[0] // 2
    first_rows = conv_split(half)
    loads = [
        [pltpu.make_async_copy(src.at[h], dst.at[h], load_sem.at[i, h]) for h in range(2)]
        for i, (src, dst) in enumerate(zip(given, stored))
    ]
    for i in range(3):
        for h in range(2):
            loads[i][h].start()
    saves = [pltpu.make_async_copy(coarse, out_coarse, save_sem.at[2, 1])]
    saves[0].start()
    for i, start, rows in ((0, 0, first_rows), (1, first_rows, half - first_rows)):
        for h in range(2):
            loads[i][h].wait()
            n = stored[i].shape[1]
            chunk = rows // n
            for q in range(n):
                full_conv[pl.ds(h * half + start + q * chunk, chunk)] = stored[i][
                    h, q, pl.ds(0, chunk)
                ].astype(F32)
            at = pl.ds(h * half + start, rows)
            saves.append(
                pltpu.make_async_copy(full_conv.at[at], out_conv.at[at], save_sem.at[i, h])
            )
            saves[-1].start()
    for h in range(2):
        loads[2][h].wait()
        full_down[:, pl.ds(h * 128, 128)] = (
            stored[2][h].reshape(full_down.shape[0], 128).astype(F32)
        )
    saves.append(pltpu.make_async_copy(full_down, out_down, save_sem.at[2, 0]))
    saves[-1].start()
    for save in saves:
        save.wait()


def body(n, nx, *args):
    args = list(args)
    args[1] = jnp.transpose(args[1], (1, 0, 2))
    features, _, _, _, cell_source, conv_weight, _, cotangent = args
    rows, width = features.shape[1:]
    offsets = conv_weight.shape[0]
    cells = cell_source.shape[1]
    cap = cells // (2 * n * n)
    half = offsets * width // 2
    first_rows = conv_split(half)
    exchange = [
        pltpu.VMEM((n, cells // n, width), BF16),
        pltpu.VMEM((n, cells // n, width), BF16),
        pltpu.VMEM((n, 2, cells // n // 2, width), BF16),
        pltpu.VMEM((n, 2, cells // n // 2, width), BF16),
        pltpu.VMEM((2, n, cells // n // 2, width), BF16),
    ]
    sizes = {"a": n, "b": n, "x": nx}
    jobs = [
        (total, *[sizes[name] for name in order])
        for total, order in zip((first_rows, half - first_rows, OCT * width), ORDERS)
    ]
    copies = 2 + 2 * (2 * (n - 1) + 1)
    copies += sum(2 + 2 * (n1 - 1) + 2 * (n2 - 1) + n3 - 1 for _, n1, n2, n3 in jobs)
    hbm = pl.BlockSpec(memory_space=pl.ANY)
    parts = pl.pallas_call(
        functools.partial(kernel, n, nx, cap),
        out_shape=[jax.ShapeDtypeStruct(cotangent.shape, BF16)]
        + [
            jax.ShapeDtypeStruct((2, n1, up16(total // n1), 128), BF16) for total, n1, _, _ in jobs
        ],
        in_specs=[hbm] * 8,
        out_specs=[hbm] * 4,
        scratch_shapes=[
            *[
                (pltpu.SMEM if i == 2 else pltpu.VMEM)(arg.shape, arg.dtype)
                for i, arg in enumerate(args)
                if i > 0
            ],
            pltpu.VMEM((rows + 2 * HALO, width), BF16),
            pltpu.VMEM((width, offsets * width), BF16),
            pltpu.VMEM((offsets * width, rows), BF16),
            pltpu.VMEM((cells, width), F32),
            pltpu.VMEM((cells, rows), BF16),
            pltpu.VMEM((cells, cells), BF16),
            pltpu.VMEM((2, OCT * width, 128), F32),
            pltpu.VMEM(cotangent.shape, BF16),
            *exchange,
            *exchange,
            *[
                ref
                for job, order in zip(jobs, ORDERS)
                for ref in Sum.scratch(*job, BF16 if order[0] == "x" else F32)
            ],
            pltpu.SemaphoreType.DMA((copies,)),
            pltpu.SemaphoreType.DMA((copies,)),
            pltpu.SemaphoreType.DMA((4,)),
            pltpu.SemaphoreType.DMA((8,)),
        ],
        compiler_params=pltpu.CompilerParams(
            collective_id=0, has_side_effects=True, vmem_limit_bytes=64 << 20
        ),
    )(*args)
    coarse, grad_conv, grad_down = pl.pallas_call(
        finish,
        out_shape=[
            jax.ShapeDtypeStruct(cotangent.shape, BF16),
            jax.ShapeDtypeStruct((offsets * width, width), F32),
            jax.ShapeDtypeStruct((OCT * width, 256), F32),
        ],
        in_specs=[hbm] * 4,
        out_specs=[hbm] * 3,
        scratch_shapes=[
            *[pltpu.VMEM(part.shape, BF16) for part in parts[1:]],
            pltpu.VMEM((offsets * width, width), F32),
            pltpu.VMEM((OCT * width, 256), F32),
            pltpu.SemaphoreType.DMA((3, 2)),
            pltpu.SemaphoreType.DMA((3, 2)),
        ],
        compiler_params=pltpu.CompilerParams(vmem_limit_bytes=64 << 20),
    )(*parts)
    return (coarse, grad_conv.reshape(offsets, width, width), grad_down)


def solution(mesh):
    n, nx = math.isqrt(mesh.shape["blk"] // 2), mesh.shape["dp"]
    in_specs = (
        P("dp", "blk", None),
        P("dp", None, "blk"),
        P("dp", None),
        P("dp", "blk"),
        P("dp", "blk"),
        P(),
        P(),
        P("dp", "blk", None),
    )
    out_specs = (P("dp", "blk", None), P(), P())
    return jax.shard_map(
        functools.partial(body, n, nx),
        mesh=mesh,
        in_specs=in_specs,
        out_specs=out_specs,
        check_vma=False,
    )
```

```python
import functools
import math

import jax
import jax.numpy as jnp
from jax import lax
from jax.experimental import pallas as pl
from jax.experimental.pallas import tpu as pltpu
from jax.sharding import PartitionSpec as P

OCT = 8
HALO = 64
F32 = jnp.float32
BF16 = jnp.bfloat16
MESH = pl.DeviceIdType.MESH


def iota(shape, dim):
    return lax.broadcasted_iota(jnp.int32, shape, dim)


def dot(a, b, ca, cb):
    return lax.dot_general(a, b, (((ca,), (cb,)), ((), ())), preferred_element_type=F32)


def up16(rows):
    return -(-rows // 16) * 16


class Place:
    def __init__(self, n, nx):
        blk = lax.axis_index("blk")
        self.n, self.nx = n, nx
        self.blk, self.x = blk, lax.axis_index("dp")
        self.c = lax.rem(blk, 2)
        chip = lax.div(blk, 2)
        z, y = lax.div(chip, n), lax.rem(chip, n)
        self.a = (1 - self.c) * y + self.c * z
        self.b = (1 - self.c) * z + self.c * y

    def of(self, a, b):
        c, n = self.c, self.n
        return ((1 - c) * (b * n + a) + c * (a * n + b)) * 2 + c

    def axis(self, name):
        if name == "x":
            return self.nx, self.x, self.along_x
        return (self.n, self.a, self.along_a) if name == "a" else (self.n, self.b, self.along_b)

    def along_a(self, p):
        return (self.of(lax.rem(self.a + p, self.n), self.b), self.x)

    def along_b(self, p):
        return (self.of(self.a, lax.rem(self.b + p, self.n)), self.x)

    def along_x(self, p):
        return (self.blk, lax.rem(self.x + p, self.nx))

    def other_core(self):
        return (self.blk + 1 - 2 * self.c, self.x)

    def next_block(self, p, count):
        return (lax.rem(self.blk + p, count), self.x)


class Sender:
    def __init__(self, send_sem, recv_sem):
        self.send_sem, self.recv_sem, self.used, self.all = send_sem, recv_sem, 0, []

    def start(self, src, dst, device):
        copy = pltpu.make_async_remote_copy(
            src_ref=src,
            dst_ref=dst,
            send_sem=self.send_sem.at[self.used],
            recv_sem=self.recv_sem.at[self.used],
            device_id=device,
            device_id_type=MESH,
        )
        self.used += 1
        copy.start()
        self.all.append(copy)
        return copy

    def finish(self, recent=0):
        old = len(self.all) - recent
        for copy in self.all[:old]:
            copy.wait_send()
        self.all = self.all[old:]


def arrived(copies):
    for copy in copies:
        copy.wait_recv()


class Exchange:
    def __init__(self, place, sender, bufs, whole):
        self.place, self.sender, self.whole = place, sender, whole
        self.send1, self.recv1, self.send2, self.recv2, self.got = bufs
        if whole:
            self.recv2 = self.got.at[place.c]

    def start(self, rows):
        pc, n = self.place, self.place.n
        self.send1[...] = rows.reshape(self.send1.shape)
        self.copies = [
            self.sender.start(
                self.send1.at[lax.rem(pc.a + p, n)], self.recv1.at[pc.a], pc.along_a(p)
            )
            for p in range(1, n)
        ]
        self.recv1[pc.a] = self.send1[pc.a]

    def second(self, swap):
        pc, n = self.place, self.place.n
        arrived(self.copies)
        flat = self.recv1[...].reshape(swap.shape[1], -1)
        moved = jnp.dot(swap[...], flat, preferred_element_type=F32).astype(BF16)
        self.send2[...] = moved.reshape(self.send2.shape)
        self.copies = [
            self.sender.start(
                self.send2.at[lax.rem(pc.b + p, n)], self.recv2.at[pc.b], pc.along_b(p)
            )
            for p in range(1, n)
        ]
        self.recv2[pc.b] = self.send2[pc.b]

    def third(self):
        pc = self.place
        arrived(self.copies)
        if self.whole:
            self.copies = [self.sender.start(self.recv2, self.recv2, pc.other_core())]
            return
        self.copies = [
            self.sender.start(self.recv2.at[:, 1 - pc.c], self.got.at[pc.c], pc.other_core())
        ]
        self.got[pc.c] = self.recv2[:, pc.c]

    def result(self):
        arrived(self.copies)
        if self.whole:
            rows = [self.got[:, :, core] for core in range(2)]
            return [flat.reshape(-1, flat.shape[-1]) for flat in rows]
        flat = self.got[...]
        return flat.reshape(-1, flat.shape[-1])


class Sum:
    def __init__(self, place, sender, rows, order, bufs, out):
        self.place, self.sender, self.out = place, sender, out
        self.axes = [place.axis(name) for name in order]
        self.rows, self.part, self.wide = self.sizes(rows, *[axis[0] for axis in self.axes[:2]])
        self.own, self.s1, self.r1, self.s2, self.r2, self.s3, self.g2, self.g1 = bufs

    @staticmethod
    def sizes(rows, n1, n2):
        chunk = rows // n1
        return chunk, up16(-(-chunk // n2)), up16(chunk)

    @staticmethod
    def scratch(rows, n1, n2, n3, middle):
        _, part, wide = Sum.sizes(rows, n1, n2)
        return [
            pltpu.VMEM((rows, 128), F32),
            pltpu.VMEM((n1, wide, 128), BF16),
            pltpu.VMEM((n1, wide, 128), BF16),
            pltpu.VMEM((n2, part, 128), middle),
            pltpu.VMEM((n2, part, 128), middle),
            pltpu.VMEM((n3, part, 128), middle),
            pltpu.VMEM((n2 * part, 128), BF16),
            pltpu.VMEM((n1, wide, 128), BF16),
        ]

    def first(self):
        (n, me, along), rows = self.axes[0], self.rows
        for q in range(n):
            self.s1[q, pl.ds(0, rows)] = self.own[pl.ds(q * rows, rows)].astype(BF16)
            if self.wide > rows:
                self.s1[q, pl.ds(rows, self.wide - rows)] = jnp.zeros(
                    (self.wide - rows, 128), BF16
                )
        self.copies = [
            self.sender.start(self.s1.at[lax.rem(me + p, n)], self.r1.at[p], along(p))
            for p in range(1, n)
        ]

    def second(self):
        (n1, me1, _), (n, me, along), rows = self.axes[0], self.axes[1], self.rows
        arrived(self.copies)
        total = self.own[pl.ds(pl.multiple_of(me1 * rows, 8), rows)]
        for p in range(1, n1):
            total += self.r1[p][:rows].astype(F32)
        spare = n * self.part - rows
        if spare:
            total = jnp.concatenate([total, jnp.zeros((spare, 128), F32)], 0)
        self.s2[...] = total.reshape(self.s2.shape).astype(self.s2.dtype)
        self.copies = [
            self.sender.start(self.s2.at[lax.rem(me + p, n)], self.r2.at[p], along(p))
            for p in range(1, n)
        ]

    def third(self):
        (n2, me2, _), (n, me, along) = self.axes[1:]
        arrived(self.copies)
        total = self.s2[me2].astype(F32)
        for p in range(1, n2):
            total += self.r2[p].astype(F32)
        self.s3[me] = total.astype(self.s3.dtype)
        self.copies = [
            self.sender.start(self.s3.at[me], self.s3.at[me], along(p)) for p in range(1, n)
        ]

    def back_second(self):
        n, me, along = self.axes[1]
        arrived(self.copies)
        total = self.s3[0].astype(F32)
        for x in range(1, self.axes[2][0]):
            total += self.s3[x].astype(F32)
        mine = pl.ds(pl.multiple_of(me * self.part, 16), self.part)
        self.g2[mine] = total.astype(BF16)
        self.copies = [
            self.sender.start(self.g2.at[mine], self.g2.at[mine], along(p)) for p in range(1, n)
        ]

    def back_first(self):
        n, me, along = self.axes[0]
        arrived(self.copies)
        self.g1[me] = self.g2[pl.ds(0, self.wide)]
        self.copies = [
            self.sender.start(self.g1.at[me], self.g1.at[me], along(p)) for p in range(1, n)
        ]

    def back_core(self, sem):
        pc = self.place
        arrived(self.copies)
        self.copies = [self.sender.start(self.g1, self.out.at[pc.c], pc.other_core())]
        self.kept = pltpu.make_async_copy(self.g1, self.out.at[pc.c], sem)
        self.kept.start()

    def result(self):
        arrived(self.copies)
        self.kept.wait()


def conv_split(rows):
    return rows * 13 // 27


ORDERS = (("a", "b", "x"), ("x", "a", "b"), ("x", "a", "b"))


def kernel(n, nx, cap, *refs):
    given, (out_coarse, *outs), refs = refs[:8], refs[8:12], refs[12:]
    (
        kernel_map,
        block_counts,
        send_position,
        conv_weight,
        down_weight,
        cell_source,
        cotangent,
        raw,
        weight_t,
        picked,
        by_child,
        send_hot,
        swap,
        coarse,
        their_raw,
        their_map,
        their_picked,
        grad_pre,
        *rest,
    ) = refs
    *rest, send_sem, recv_sem, local_sem, load_sem = rest
    count = 2 * n * n
    features = given[0]
    offsets = conv_weight.shape[0]
    rows, width = features.shape[1], features.shape[2]
    cells = count * cap
    half = offsets * width // 2
    pc = Place(n, nx)
    sender = Sender(send_sem, recv_sem)

    barrier = pltpu.get_barrier_semaphore()
    partners = [pc.along_a(p) for p in range(1, n)] + [pc.along_b(p) for p in range(1, n)]
    partners += [pc.along_x(p) for p in range(1, nx)]
    partners += [pc.other_core(), pc.next_block(1, count), pc.next_block(count - 1, count)]
    for device in partners:
        pl.semaphore_signal(barrier, inc=1, device_id=device, device_id_type=MESH)

    sources = [features.at[0], *given[1:7], given[7].at[0]]
    targets = [raw.at[pl.ds(HALO, rows)], kernel_map, block_counts, send_position]
    targets += [cell_source.at[pc.c], conv_weight, down_weight, cotangent.at[pc.c]]
    loads = [
        pltpu.make_async_copy(src, dst, load_sem.at[i])
        for i, (src, dst) in enumerate(zip(sources, targets))
    ]
    for i in (7, 6, 4, 0, 2, 3, 1, 5):
        loads[i].start()
    pl.semaphore_wait(barrier, len(partners))

    halo = [
        sender.start(
            features.at[0, pl.ds(rows - HALO, HALO)],
            raw.at[pl.ds(0, HALO)],
            pc.next_block(1, count),
        ),
        sender.start(
            features.at[0, pl.ds(0, HALO)],
            raw.at[pl.ds(HALO + rows, HALO)],
            pc.next_block(count - 1, count),
        ),
    ]
    shared = [
        sender.start(given[4], cell_source.at[pc.c], pc.other_core()),
        sender.start(given[7].at[0], cotangent.at[pc.c], pc.other_core()),
    ]
    shared_map = sender.start(given[1], their_map, pc.other_core())

    forward = Exchange(pc, sender, rest[0:5], True)
    backward = Exchange(pc, sender, rest[5:10], False)
    first_rows = conv_split(half)
    sums = [
        Sum(pc, sender, total, order, rest[10 + 8 * i : 18 + 8 * i], outs[i])
        for i, (total, order) in enumerate(
            zip((first_rows, half - first_rows, OCT * width), ORDERS)
        )
    ]
    sum_conv, sum_down = sums[:2], sums[2]

    r = iota((cells, 1), 0)
    slot, r1 = lax.rem(r, cap), lax.div(r, cap)
    to_b, r2 = lax.rem(r1, n), lax.div(r1, n)
    to_c, to_a = lax.rem(r2, 2), lax.div(r2, 2)
    chip = jnp.where(pc.c == 0, to_b * n + to_a, to_a * n + to_b)
    goes_to = (chip * 2 + to_c) * cap + slot
    from_a, from_b, from_c = to_b, lax.rem(r2, n), lax.div(r2, n)
    chip = jnp.where(from_c == 0, from_b * n + from_a, from_a * n + from_b)
    comes_from = (chip * 2 + from_c) * cap + slot

    def hot(at, values):
        return jnp.where(at == values, 1.0, 0.0).astype(BF16)

    for i in (7, 6, 4):
        loads[i].wait()
    for j in range(OCT):
        part = dot(cotangent[pc.c], down_weight[pl.ds(j * width, width)], 1, 1)
        by_child[0, pl.ds(j, rows // 4, stride=OCT)] = part.astype(BF16).astype(F32)
    backward.start(
        jnp.dot(
            hot(goes_to, cell_source[pc.c]),
            by_child[0].astype(BF16),
            preferred_element_type=F32,
        ).astype(BF16)
    )

    loads[0].wait()
    loads[2].wait()

    def live_of(block, inside):
        counted = block_counts[0, lax.rem(block, count)]
        front = lax.div(counted, 2)
        return (inside < front) | (inside >= rows - (counted - front))

    loads[5].wait()
    for k in range(offsets):
        weight_t[:, pl.ds(k * width, width)] = conv_weight[k].astype(F32).T.astype(BF16)
    loads[1].wait()
    lane = lax.rem(iota((1, rows), 1), 128)
    window = iota((2 * HALO + 128, 128), 0)
    live_t = live_of(pc.blk, iota((1, rows), 1))

    def table_of(block, ref):
        live = jnp.concatenate(
            [
                live_of(block + count - 1, iota((HALO, width), 0) + rows - HALO),
                live_of(block, iota((rows, width), 0)),
                live_of(block + 1, iota((HALO, width), 0)),
            ],
            0,
        )
        return jnp.where(live, ref[...].astype(F32), 0.0).T.astype(BF16)

    def pick(table_t, entry, k, ref):
        index = jnp.where(entry >= 0, entry + lane, -1)
        for t in range(rows // 128):
            chosen = hot(window, index[:, t * 128 : (t + 1) * 128])
            got = jnp.dot(
                table_t[:, t * 128 : t * 128 + 128 + 2 * HALO], chosen, preferred_element_type=F32
            )
            ref[pl.ds(k * width, width), pl.ds(t * 128, 128)] = got.astype(BF16)

    arrived(halo)
    shared_raw = sender.start(raw, their_raw, pc.other_core())
    table_t = table_of(pc.blk, raw)
    for k in range(offsets):
        pick(table_t, kernel_map[k], k, picked)

    loads[3].wait()
    position = send_position[...]
    send_hot[...] = hot(goes_to, position)
    pre = jnp.dot(weight_t[...], picked[...], preferred_element_type=F32)
    sig = 1.0 / (1.0 + jnp.exp(-pre))
    hidden = jnp.where(live_t, pre * sig, 0.0).astype(BF16)
    forward.start(dot(send_hot[...], hidden, 1, 1).astype(BF16))

    swapped = ((to_b * 2 + to_c) * n + to_a) * cap + slot
    swap[...] = hot(swapped, iota((1, cells), 1))
    backward.second(swap)
    from_owner = hot(comes_from, position)
    slope = jnp.where(live_t, sig * (1.0 + pre * (1.0 - sig)), 0.0)

    arrived([shared_map, shared_raw])
    skipped = offsets // 2
    table_t = table_of(pc.blk + 1 - 2 * pc.c, their_raw)
    for k in range(offsets - skipped):
        pick(table_t, their_map[pc.c * skipped + k], k, their_picked)

    forward.second(swap)
    backward.third()
    grad_hidden = dot(backward.result(), from_owner, 0, 0)
    grad_pre[pc.c] = (grad_hidden * slope).astype(BF16)
    shared_grad = sender.start(grad_pre.at[pc.c], grad_pre.at[pc.c], pc.other_core())
    splits = (
        (sum_conv[0], 0, first_rows),
        (sum_conv[1], first_rows, half - first_rows),
    )
    for job, start, size in splits:
        mine = picked[pl.ds(pl.multiple_of(pc.c * half + start, 16), size)]
        job.own[...] = dot(mine, grad_pre[pc.c], 1, 1)
    arrived([shared_grad])
    for job, start, size in splits:
        at = pc.c * (half - skipped * width) + start
        theirs = their_picked[pl.ds(pl.multiple_of(at, 16), size)]
        job.own[...] += dot(theirs, grad_pre[1 - pc.c], 1, 1)
        job.first()
    forward.third()

    arrived(shared)
    for core, incoming in enumerate(forward.result()):
        by_child[core] = dot(hot(comes_from, cell_source[core]), incoming, 0, 0)
    quarter = rows // 4
    mine = pl.ds(pl.multiple_of(pc.c * 128, 128), 128)
    wanted = jnp.concatenate([cotangent[core, :, mine] for core in range(2)], 0)
    for j in range(OCT):
        child = [by_child[core, pl.ds(j, quarter, stride=OCT)] for core in range(2)]
        child = jnp.concatenate(child, 0).astype(BF16)
        sum_down.own[pl.ds(j * width, width)] = dot(child, wanted, 0, 0)
    sum_down.first()
    total = jnp.zeros(coarse.shape[1:], F32)
    for j in range(OCT):
        child = by_child[pc.c, pl.ds(j, quarter, stride=OCT)].astype(BF16)
        total += jnp.dot(
            child, down_weight[pl.ds(j * width, width)], preferred_element_type=F32
        )
    coarse[0] = total.astype(BF16)
    kept = pltpu.make_async_copy(coarse, out_coarse, local_sem.at[3])
    kept.start()

    for job in sums:
        job.second()
    for job in sums:
        job.third()
    for job in sums:
        job.back_second()
    sent = len(sender.all)
    for job in sums:
        job.back_first()
    sender.finish(len(sender.all) - sent)
    for i, job in enumerate(sums):
        job.back_core(local_sem.at[i])
    kept.wait()
    sender.finish(len(sums))
    for job in sums:
        job.result()
    sender.finish()


def finish(coarse, conv_a, conv_x, down, out_coarse, out_conv, out_down, *refs):
    *stored, full_conv, full_down, load_sem, save_sem = refs
    given = (conv_a, conv_x, down)
    half = out_conv.shape[0] // 2
    first_rows = conv_split(half)
    loads = [
        [pltpu.make_async_copy(src.at[h], dst.at[h], load_sem.at[i, h]) for h in range(2)]
        for i, (src, dst) in enumerate(zip(given, stored))
    ]
    for i in range(3):
        for h in range(2):
            loads[i][h].start()
    saves = [pltpu.make_async_copy(coarse, out_coarse, save_sem.at[2, 1])]
    saves[0].start()
    for i, start, rows in ((0, 0, first_rows), (1, first_rows, half - first_rows)):
        for h in range(2):
            loads[i][h].wait()
            n = stored[i].shape[1]
            chunk = rows // n
            for q in range(n):
                full_conv[pl.ds(h * half + start + q * chunk, chunk)] = stored[i][
                    h, q, pl.ds(0, chunk)
                ].astype(F32)
            at = pl.ds(h * half + start, rows)
            saves.append(
                pltpu.make_async_copy(full_conv.at[at], out_conv.at[at], save_sem.at[i, h])
            )
            saves[-1].start()
    for h in range(2):
        loads[2][h].wait()
        full_down[:, pl.ds(h * 128, 128)] = (
            stored[2][h].reshape(full_down.shape[0], 128).astype(F32)
        )
    saves.append(pltpu.make_async_copy(full_down, out_down, save_sem.at[2, 0]))
    saves[-1].start()
    for save in saves:
        save.wait()


def body(n, nx, *args):
    args = list(args)
    args[1] = jnp.transpose(args[1], (1, 0, 2))
    features, _, _, _, cell_source, conv_weight, _, cotangent = args
    rows, width = features.shape[1:]
    offsets = conv_weight.shape[0]
    cells = cell_source.shape[1]
    cap = cells // (2 * n * n)
    half = offsets * width // 2
    first_rows = conv_split(half)
    exchange = [
        pltpu.VMEM((n, cells // n, width), BF16),
        pltpu.VMEM((n, cells // n, width), BF16),
        pltpu.VMEM((n, 2, cells // n // 2, width), BF16),
        pltpu.VMEM((n, 2, cells // n // 2, width), BF16),
    ]
    one = pltpu.VMEM((2, n, cells // n // 2, width), BF16)
    both = pltpu.VMEM((2, n, 2, cells // n // 2, width), BF16)
    sizes = {"a": n, "b": n, "x": nx}
    jobs = [
        (total, *[sizes[name] for name in order])
        for total, order in zip((first_rows, half - first_rows, OCT * width), ORDERS)
    ]
    copies = 7 + 2 * (2 * (n - 1) + 1)
    copies += sum(1 + 2 * (n1 - 1) + 2 * (n2 - 1) + n3 - 1 for _, n1, n2, n3 in jobs)
    hbm = pl.BlockSpec(memory_space=pl.ANY)
    parts = pl.pallas_call(
        functools.partial(kernel, n, nx, cap),
        out_shape=[jax.ShapeDtypeStruct(cotangent.shape, BF16)]
        + [
            jax.ShapeDtypeStruct((2, n1, up16(total // n1), 128), BF16) for total, n1, _, _ in jobs
        ],
        in_specs=[hbm] * 8,
        out_specs=[hbm] * 4,
        scratch_shapes=[
            *[
                (pltpu.SMEM if i == 2 else pltpu.VMEM)(args[i].shape, args[i].dtype)
                for i in (1, 2, 3, 5, 6)
            ],
            pltpu.VMEM((2, 1, cells), jnp.int32),
            pltpu.VMEM((2, *cotangent.shape[1:]), BF16),
            pltpu.VMEM((rows + 2 * HALO, width), BF16),
            pltpu.VMEM((width, offsets * width), BF16),
            pltpu.VMEM((offsets * width, rows), BF16),
            pltpu.VMEM((2, cells, width), F32),
            pltpu.VMEM((cells, rows), BF16),
            pltpu.VMEM((cells, cells), BF16),
            pltpu.VMEM(cotangent.shape, BF16),
            pltpu.VMEM((rows + 2 * HALO, width), BF16),
            pltpu.VMEM(args[1].shape, jnp.int32),
            pltpu.VMEM(((offsets - offsets // 2) * width, rows), BF16),
            pltpu.VMEM((2, width, rows), BF16),
            *exchange,
            both,
            *exchange,
            one,
            *[
                ref
                for job, order in zip(jobs, ORDERS)
                for ref in Sum.scratch(*job, BF16 if order[0] == "x" else F32)
            ],
            pltpu.SemaphoreType.DMA((copies,)),
            pltpu.SemaphoreType.DMA((copies,)),
            pltpu.SemaphoreType.DMA((4,)),
            pltpu.SemaphoreType.DMA((8,)),
        ],
        compiler_params=pltpu.CompilerParams(
            collective_id=0, has_side_effects=True, vmem_limit_bytes=64 << 20
        ),
    )(*args)
    coarse, grad_conv, grad_down = pl.pallas_call(
        finish,
        out_shape=[
            jax.ShapeDtypeStruct(cotangent.shape, BF16),
            jax.ShapeDtypeStruct((offsets * width, width), F32),
            jax.ShapeDtypeStruct((OCT * width, 256), F32),
        ],
        in_specs=[hbm] * 4,
        out_specs=[hbm] * 3,
        scratch_shapes=[
            *[pltpu.VMEM(part.shape, BF16) for part in parts[1:]],
            pltpu.VMEM((offsets * width, width), F32),
            pltpu.VMEM((OCT * width, 256), F32),
            pltpu.SemaphoreType.DMA((3, 2)),
            pltpu.SemaphoreType.DMA((3, 2)),
        ],
        compiler_params=pltpu.CompilerParams(vmem_limit_bytes=64 << 20),
    )(*parts)
    return (coarse, grad_conv.reshape(offsets, width, width), grad_down)


def solution(mesh):
    n, nx = math.isqrt(mesh.shape["blk"] // 2), mesh.shape["dp"]
    in_specs = (
        P("dp", "blk", None),
        P("dp", None, "blk"),
        P("dp", None),
        P("dp", "blk"),
        P("dp", "blk"),
        P(),
        P(),
        P("dp", "blk", None),
    )
    out_specs = (P("dp", "blk", None), P(), P())
    return jax.shard_map(
        functools.partial(body, n, nx),
        mesh=mesh,
        in_specs=in_specs,
        out_specs=out_specs,
        check_vma=False,
    )
```

```python
import functools
import math

import jax
import jax.numpy as jnp
from jax import lax
from jax.experimental import pallas as pl
from jax.experimental.pallas import tpu as pltpu
from jax.sharding import PartitionSpec as P

OCT = 8
HALO = 64
F32 = jnp.float32
BF16 = jnp.bfloat16
MESH = pl.DeviceIdType.MESH


def iota(shape, dim):
    return lax.broadcasted_iota(jnp.int32, shape, dim)


def dot(a, b, ca, cb):
    return lax.dot_general(a, b, (((ca,), (cb,)), ((), ())), preferred_element_type=F32)


def up16(rows):
    return -(-rows // 16) * 16


def far_first(n):
    return sorted(range(1, n), key=lambda p: -min(p, n - p))


class Place:
    def __init__(self, n, nx):
        blk = lax.axis_index("blk")
        self.n, self.nx = n, nx
        self.blk, self.x = blk, lax.axis_index("dp")
        self.c = lax.rem(blk, 2)
        chip = lax.div(blk, 2)
        z, y = lax.div(chip, n), lax.rem(chip, n)
        self.a = (1 - self.c) * y + self.c * z
        self.b = (1 - self.c) * z + self.c * y

    def of(self, a, b):
        c, n = self.c, self.n
        return ((1 - c) * (b * n + a) + c * (a * n + b)) * 2 + c

    def axis(self, name):
        if name == "x":
            return self.nx, self.x, self.along_x
        return (self.n, self.a, self.along_a) if name == "a" else (self.n, self.b, self.along_b)

    def along_a(self, p):
        return (self.of(lax.rem(self.a + p, self.n), self.b), self.x)

    def along_b(self, p):
        return (self.of(self.a, lax.rem(self.b + p, self.n)), self.x)

    def along_x(self, p):
        return (self.blk, lax.rem(self.x + p, self.nx))

    def other_core(self):
        return (self.blk + 1 - 2 * self.c, self.x)

    def next_block(self, p, count):
        return (lax.rem(self.blk + p, count), self.x)


class Sender:
    def __init__(self, send_sem, recv_sem):
        self.send_sem, self.recv_sem, self.used, self.all = send_sem, recv_sem, 0, []

    def start(self, src, dst, device):
        copy = pltpu.make_async_remote_copy(
            src_ref=src,
            dst_ref=dst,
            send_sem=self.send_sem.at[self.used],
            recv_sem=self.recv_sem.at[self.used],
            device_id=device,
            device_id_type=MESH,
        )
        self.used += 1
        copy.start()
        self.all.append(copy)
        return copy

    def finish(self, recent=0):
        old = len(self.all) - recent
        for copy in self.all[:old]:
            copy.wait_send()
        self.all = self.all[old:]


def arrived(copies):
    for copy in copies:
        copy.wait_recv()


class Exchange:
    def __init__(self, place, sender, bufs, whole):
        self.place, self.sender, self.whole = place, sender, whole
        self.send1, self.recv1, self.send2, self.recv2, self.got = bufs
        if whole:
            self.recv2 = self.got.at[place.c]

    def start(self, rows):
        pc, n = self.place, self.place.n
        self.send1[...] = rows.reshape(self.send1.shape)
        self.copies = [
            self.sender.start(
                self.send1.at[lax.rem(pc.a + p, n)], self.recv1.at[pc.a], pc.along_a(p)
            )
            for p in far_first(n)
        ]
        self.recv1[pc.a] = self.send1[pc.a]

    def second(self, swap):
        pc, n = self.place, self.place.n
        arrived(self.copies)
        flat = self.recv1[...].reshape(swap.shape[1], -1)
        moved = jnp.dot(swap[...], flat, preferred_element_type=F32).astype(BF16)
        self.send2[...] = moved.reshape(self.send2.shape)
        self.copies = [
            self.sender.start(
                self.send2.at[lax.rem(pc.b + p, n)], self.recv2.at[pc.b], pc.along_b(p)
            )
            for p in far_first(n)
        ]
        self.recv2[pc.b] = self.send2[pc.b]

    def third(self):
        pc = self.place
        arrived(self.copies)
        if self.whole:
            self.copies = [self.sender.start(self.recv2, self.recv2, pc.other_core())]
            return
        self.copies = [
            self.sender.start(self.recv2.at[:, 1 - pc.c], self.got.at[pc.c], pc.other_core())
        ]
        self.got[pc.c] = self.recv2[:, pc.c]

    def result(self):
        arrived(self.copies)
        if self.whole:
            rows = [self.got[:, :, core] for core in range(2)]
            return [flat.reshape(-1, flat.shape[-1]) for flat in rows]
        flat = self.got[...]
        return flat.reshape(-1, flat.shape[-1])


class Sum:
    def __init__(self, place, sender, rows, order, bufs, out):
        self.place, self.sender, self.out = place, sender, out
        self.axes = [place.axis(name) for name in order]
        self.rows, self.part, self.wide = self.sizes(rows, *[axis[0] for axis in self.axes[:2]])
        self.own, self.s1, self.r1, self.s2, self.r2, self.s3, self.g2, self.g1 = bufs

    @staticmethod
    def sizes(rows, n1, n2):
        chunk = rows // n1
        return chunk, up16(-(-chunk // n2)), up16(chunk)

    @staticmethod
    def scratch(rows, n1, n2, n3, middle):
        _, part, wide = Sum.sizes(rows, n1, n2)
        return [
            pltpu.VMEM((rows, 128), F32),
            pltpu.VMEM((n1, wide, 128), BF16),
            pltpu.VMEM((n1, wide, 128), BF16),
            pltpu.VMEM((n2, part, 128), middle),
            pltpu.VMEM((n2, part, 128), middle),
            pltpu.VMEM((n3, part, 128), middle),
            pltpu.VMEM((n2 * part, 128), BF16),
            pltpu.VMEM((n1, wide, 128), BF16),
        ]

    def first(self):
        (n, me, along), rows = self.axes[0], self.rows
        for q in range(n):
            self.s1[q, pl.ds(0, rows)] = self.own[pl.ds(q * rows, rows)].astype(BF16)
            if self.wide > rows:
                self.s1[q, pl.ds(rows, self.wide - rows)] = jnp.zeros(
                    (self.wide - rows, 128), BF16
                )
        self.copies = [
            self.sender.start(self.s1.at[lax.rem(me + p, n)], self.r1.at[p], along(p))
            for p in far_first(n)
        ]

    def second(self):
        (n1, me1, _), (n, me, along), rows = self.axes[0], self.axes[1], self.rows
        arrived(self.copies)
        total = self.own[pl.ds(pl.multiple_of(me1 * rows, 8), rows)]
        for p in range(1, n1):
            total += self.r1[p][:rows].astype(F32)
        spare = n * self.part - rows
        if spare:
            total = jnp.concatenate([total, jnp.zeros((spare, 128), F32)], 0)
        self.s2[...] = total.reshape(self.s2.shape).astype(self.s2.dtype)
        self.copies = [
            self.sender.start(self.s2.at[lax.rem(me + p, n)], self.r2.at[p], along(p))
            for p in far_first(n)
        ]

    def third(self):
        (n2, me2, _), (n, me, along) = self.axes[1:]
        arrived(self.copies)
        total = self.s2[me2].astype(F32)
        for p in range(1, n2):
            total += self.r2[p].astype(F32)
        self.s3[me] = total.astype(self.s3.dtype)
        self.copies = [
            self.sender.start(self.s3.at[me], self.s3.at[me], along(p)) for p in far_first(n)
        ]

    def back_second(self):
        n, me, along = self.axes[1]
        arrived(self.copies)
        total = self.s3[0].astype(F32)
        for x in range(1, self.axes[2][0]):
            total += self.s3[x].astype(F32)
        mine = pl.ds(pl.multiple_of(me * self.part, 16), self.part)
        self.g2[mine] = total.astype(BF16)
        self.copies = [
            self.sender.start(self.g2.at[mine], self.g2.at[mine], along(p)) for p in far_first(n)
        ]

    def back_first(self):
        n, me, along = self.axes[0]
        arrived(self.copies)
        self.g1[me] = self.g2[pl.ds(0, self.wide)]
        self.copies = [
            self.sender.start(self.g1.at[me], self.g1.at[me], along(p)) for p in far_first(n)
        ]

    def back_core(self, sem):
        pc = self.place
        arrived(self.copies)
        self.copies = [self.sender.start(self.g1, self.out.at[pc.c], pc.other_core())]
        self.kept = pltpu.make_async_copy(self.g1, self.out.at[pc.c], sem)
        self.kept.start()

    def result(self):
        arrived(self.copies)
        self.kept.wait()


def conv_split(rows):
    return rows * 13 // 27


ORDERS = (("a", "b", "x"), ("x", "a", "b"), ("x", "a", "b"))


def kernel(n, nx, cap, *refs):
    given, (out_coarse, *outs), refs = refs[:8], refs[8:12], refs[12:]
    (
        kernel_map,
        block_counts,
        send_position,
        conv_weight,
        down_weight,
        cell_source,
        cotangent,
        raw,
        weight_t,
        picked,
        by_child,
        send_hot,
        swap,
        coarse,
        their_raw,
        their_map,
        their_picked,
        grad_pre,
        *rest,
    ) = refs
    *rest, send_sem, recv_sem, local_sem, load_sem = rest
    count = 2 * n * n
    features = given[0]
    offsets = conv_weight.shape[0]
    rows, width = features.shape[1], features.shape[2]
    cells = count * cap
    half = offsets * width // 2
    pc = Place(n, nx)
    sender = Sender(send_sem, recv_sem)

    barrier = pltpu.get_barrier_semaphore()
    partners = [pc.along_a(p) for p in range(1, n)] + [pc.along_b(p) for p in range(1, n)]
    partners += [pc.along_x(p) for p in range(1, nx)]
    partners += [pc.other_core(), pc.next_block(1, count), pc.next_block(count - 1, count)]
    for device in partners:
        pl.semaphore_signal(barrier, inc=1, device_id=device, device_id_type=MESH)

    sources = [features.at[0], *given[1:7], given[7].at[0]]
    targets = [raw.at[pl.ds(HALO, rows)], kernel_map, block_counts, send_position]
    targets += [cell_source.at[pc.c], conv_weight, down_weight, cotangent.at[pc.c]]
    loads = [
        pltpu.make_async_copy(src, dst, load_sem.at[i])
        for i, (src, dst) in enumerate(zip(sources, targets))
    ]
    for i in (7, 6, 4, 0, 2, 3, 1, 5):
        loads[i].start()
    pl.semaphore_wait(barrier, len(partners))

    halo = [
        sender.start(
            features.at[0, pl.ds(rows - HALO, HALO)],
            raw.at[pl.ds(0, HALO)],
            pc.next_block(1, count),
        ),
        sender.start(
            features.at[0, pl.ds(0, HALO)],
            raw.at[pl.ds(HALO + rows, HALO)],
            pc.next_block(count - 1, count),
        ),
    ]
    shared = [
        sender.start(given[4], cell_source.at[pc.c], pc.other_core()),
        sender.start(given[7].at[0], cotangent.at[pc.c], pc.other_core()),
    ]
    shared_map = sender.start(given[1], their_map, pc.other_core())

    forward = Exchange(pc, sender, rest[0:5], True)
    backward = Exchange(pc, sender, rest[5:10], False)
    first_rows = conv_split(half)
    sums = [
        Sum(pc, sender, total, order, rest[10 + 8 * i : 18 + 8 * i], outs[i])
        for i, (total, order) in enumerate(
            zip((first_rows, half - first_rows, OCT * width), ORDERS)
        )
    ]
    sum_conv, sum_down = sums[:2], sums[2]

    r = iota((cells, 1), 0)
    slot, r1 = lax.rem(r, cap), lax.div(r, cap)
    to_b, r2 = lax.rem(r1, n), lax.div(r1, n)
    to_c, to_a = lax.rem(r2, 2), lax.div(r2, 2)
    chip = jnp.where(pc.c == 0, to_b * n + to_a, to_a * n + to_b)
    goes_to = (chip * 2 + to_c) * cap + slot
    from_a, from_b, from_c = to_b, lax.rem(r2, n), lax.div(r2, n)
    chip = jnp.where(from_c == 0, from_b * n + from_a, from_a * n + from_b)
    comes_from = (chip * 2 + from_c) * cap + slot

    def hot(at, values):
        return jnp.where(at == values, 1.0, 0.0).astype(BF16)

    for i in (7, 6, 4):
        loads[i].wait()
    for j in range(OCT):
        part = dot(cotangent[pc.c], down_weight[pl.ds(j * width, width)], 1, 1)
        by_child[0, pl.ds(j, rows // 4, stride=OCT)] = part.astype(BF16).astype(F32)
    backward.start(
        jnp.dot(
            hot(goes_to, cell_source[pc.c]),
            by_child[0].astype(BF16),
            preferred_element_type=F32,
        ).astype(BF16)
    )

    loads[0].wait()
    loads[2].wait()

    def live_of(block, inside):
        counted = block_counts[0, lax.rem(block, count)]
        front = lax.div(counted, 2)
        return (inside < front) | (inside >= rows - (counted - front))

    loads[5].wait()
    for k in range(offsets):
        weight_t[:, pl.ds(k * width, width)] = conv_weight[k].astype(F32).T.astype(BF16)
    loads[1].wait()
    lane = lax.rem(iota((1, rows), 1), 128)
    window = iota((2 * HALO + 128, 128), 0)
    live_t = live_of(pc.blk, iota((1, rows), 1))

    def table_of(block, ref):
        live = jnp.concatenate(
            [
                live_of(block + count - 1, iota((HALO, width), 0) + rows - HALO),
                live_of(block, iota((rows, width), 0)),
                live_of(block + 1, iota((HALO, width), 0)),
            ],
            0,
        )
        return jnp.where(live, ref[...].astype(F32), 0.0).T.astype(BF16)

    def pick(table_t, entry, k, ref):
        index = jnp.where(entry >= 0, entry + lane, -1)
        for t in range(rows // 128):
            chosen = hot(window, index[:, t * 128 : (t + 1) * 128])
            got = jnp.dot(
                table_t[:, t * 128 : t * 128 + 128 + 2 * HALO], chosen, preferred_element_type=F32
            )
            ref[pl.ds(k * width, width), pl.ds(t * 128, 128)] = got.astype(BF16)

    arrived(halo)
    shared_raw = sender.start(raw, their_raw, pc.other_core())
    table_t = table_of(pc.blk, raw)
    for k in range(offsets):
        pick(table_t, kernel_map[k], k, picked)

    loads[3].wait()
    position = send_position[...]
    send_hot[...] = hot(goes_to, position)
    pre = jnp.dot(weight_t[...], picked[...], preferred_element_type=F32)
    sig = 1.0 / (1.0 + jnp.exp(-pre))
    hidden = jnp.where(live_t, pre * sig, 0.0).astype(BF16)
    forward.start(dot(send_hot[...], hidden, 1, 1).astype(BF16))

    swapped = ((to_b * 2 + to_c) * n + to_a) * cap + slot
    swap[...] = hot(swapped, iota((1, cells), 1))
    backward.second(swap)
    from_owner = hot(comes_from, position)
    slope = jnp.where(live_t, sig * (1.0 + pre * (1.0 - sig)), 0.0)

    arrived([shared_map, shared_raw])
    skipped = offsets // 2
    table_t = table_of(pc.blk + 1 - 2 * pc.c, their_raw)
    for k in range(offsets - skipped):
        pick(table_t, their_map[pc.c * skipped + k], k, their_picked)

    forward.second(swap)
    backward.third()
    grad_hidden = dot(backward.result(), from_owner, 0, 0)
    grad_pre[pc.c] = (grad_hidden * slope).astype(BF16)
    shared_grad = sender.start(grad_pre.at[pc.c], grad_pre.at[pc.c], pc.other_core())
    splits = (
        (sum_conv[0], 0, first_rows),
        (sum_conv[1], first_rows, half - first_rows),
    )
    for job, start, size in splits:
        mine = picked[pl.ds(pl.multiple_of(pc.c * half + start, 16), size)]
        job.own[...] = dot(mine, grad_pre[pc.c], 1, 1)
    arrived([shared_grad])
    for job, start, size in splits:
        at = pc.c * (half - skipped * width) + start
        theirs = their_picked[pl.ds(pl.multiple_of(at, 16), size)]
        job.own[...] += dot(theirs, grad_pre[1 - pc.c], 1, 1)
        job.first()
    forward.third()

    arrived(shared)
    for core, incoming in enumerate(forward.result()):
        by_child[core] = dot(hot(comes_from, cell_source[core]), incoming, 0, 0)
    quarter = rows // 4
    mine = pl.ds(pl.multiple_of(pc.c * 128, 128), 128)
    wanted = jnp.concatenate([cotangent[core, :, mine] for core in range(2)], 0)
    for j in range(OCT):
        child = [by_child[core, pl.ds(j, quarter, stride=OCT)] for core in range(2)]
        child = jnp.concatenate(child, 0).astype(BF16)
        sum_down.own[pl.ds(j * width, width)] = dot(child, wanted, 0, 0)
    sum_down.first()
    total = jnp.zeros(coarse.shape[1:], F32)
    for j in range(OCT):
        child = by_child[pc.c, pl.ds(j, quarter, stride=OCT)].astype(BF16)
        total += jnp.dot(
            child, down_weight[pl.ds(j * width, width)], preferred_element_type=F32
        )
    coarse[0] = total.astype(BF16)
    kept = pltpu.make_async_copy(coarse, out_coarse, local_sem.at[3])
    kept.start()

    for job in sums:
        job.second()
    for job in sums:
        job.third()
    for job in sums:
        job.back_second()
    sent = len(sender.all)
    for job in sums:
        job.back_first()
    sender.finish(len(sender.all) - sent)
    for i, job in enumerate(sums):
        job.back_core(local_sem.at[i])
    kept.wait()
    sender.finish(len(sums))
    for job in sums:
        job.result()
    sender.finish()


def finish(coarse, conv_a, conv_x, down, out_coarse, out_conv, out_down, *refs):
    *stored, full_conv, full_down, load_sem, save_sem = refs
    given = (conv_a, conv_x, down)
    half = out_conv.shape[0] // 2
    first_rows = conv_split(half)
    loads = [
        [pltpu.make_async_copy(src.at[h], dst.at[h], load_sem.at[i, h]) for h in range(2)]
        for i, (src, dst) in enumerate(zip(given, stored))
    ]
    for i in range(3):
        for h in range(2):
            loads[i][h].start()
    saves = [pltpu.make_async_copy(coarse, out_coarse, save_sem.at[2, 1])]
    saves[0].start()
    for i, start, rows in ((0, 0, first_rows), (1, first_rows, half - first_rows)):
        for h in range(2):
            loads[i][h].wait()
            n = stored[i].shape[1]
            chunk = rows // n
            for q in range(n):
                full_conv[pl.ds(h * half + start + q * chunk, chunk)] = stored[i][
                    h, q, pl.ds(0, chunk)
                ].astype(F32)
            at = pl.ds(h * half + start, rows)
            saves.append(
                pltpu.make_async_copy(full_conv.at[at], out_conv.at[at], save_sem.at[i, h])
            )
            saves[-1].start()
    for h in range(2):
        loads[2][h].wait()
        full_down[:, pl.ds(h * 128, 128)] = (
            stored[2][h].reshape(full_down.shape[0], 128).astype(F32)
        )
    saves.append(pltpu.make_async_copy(full_down, out_down, save_sem.at[2, 0]))
    saves[-1].start()
    for save in saves:
        save.wait()


def body(n, nx, *args):
    args = list(args)
    args[1] = jnp.transpose(args[1], (1, 0, 2))
    features, _, _, _, cell_source, conv_weight, _, cotangent = args
    rows, width = features.shape[1:]
    offsets = conv_weight.shape[0]
    cells = cell_source.shape[1]
    cap = cells // (2 * n * n)
    half = offsets * width // 2
    first_rows = conv_split(half)
    exchange = [
        pltpu.VMEM((n, cells // n, width), BF16),
        pltpu.VMEM((n, cells // n, width), BF16),
        pltpu.VMEM((n, 2, cells // n // 2, width), BF16),
        pltpu.VMEM((n, 2, cells // n // 2, width), BF16),
    ]
    one = pltpu.VMEM((2, n, cells // n // 2, width), BF16)
    both = pltpu.VMEM((2, n, 2, cells // n // 2, width), BF16)
    sizes = {"a": n, "b": n, "x": nx}
    jobs = [
        (total, *[sizes[name] for name in order])
        for total, order in zip((first_rows, half - first_rows, OCT * width), ORDERS)
    ]
    copies = 7 + 2 * (2 * (n - 1) + 1)
    copies += sum(1 + 2 * (n1 - 1) + 2 * (n2 - 1) + n3 - 1 for _, n1, n2, n3 in jobs)
    hbm = pl.BlockSpec(memory_space=pl.ANY)
    parts = pl.pallas_call(
        functools.partial(kernel, n, nx, cap),
        out_shape=[jax.ShapeDtypeStruct(cotangent.shape, BF16)]
        + [
            jax.ShapeDtypeStruct((2, n1, up16(total // n1), 128), BF16) for total, n1, _, _ in jobs
        ],
        in_specs=[hbm] * 8,
        out_specs=[hbm] * 4,
        scratch_shapes=[
            *[
                (pltpu.SMEM if i == 2 else pltpu.VMEM)(args[i].shape, args[i].dtype)
                for i in (1, 2, 3, 5, 6)
            ],
            pltpu.VMEM((2, 1, cells), jnp.int32),
            pltpu.VMEM((2, *cotangent.shape[1:]), BF16),
            pltpu.VMEM((rows + 2 * HALO, width), BF16),
            pltpu.VMEM((width, offsets * width), BF16),
            pltpu.VMEM((offsets * width, rows), BF16),
            pltpu.VMEM((2, cells, width), F32),
            pltpu.VMEM((cells, rows), BF16),
            pltpu.VMEM((cells, cells), BF16),
            pltpu.VMEM(cotangent.shape, BF16),
            pltpu.VMEM((rows + 2 * HALO, width), BF16),
            pltpu.VMEM(args[1].shape, jnp.int32),
            pltpu.VMEM(((offsets - offsets // 2) * width, rows), BF16),
            pltpu.VMEM((2, width, rows), BF16),
            *exchange,
            both,
            *exchange,
            one,
            *[
                ref
                for job, order in zip(jobs, ORDERS)
                for ref in Sum.scratch(*job, BF16 if order[0] == "x" else F32)
            ],
            pltpu.SemaphoreType.DMA((copies,)),
            pltpu.SemaphoreType.DMA((copies,)),
            pltpu.SemaphoreType.DMA((4,)),
            pltpu.SemaphoreType.DMA((8,)),
        ],
        compiler_params=pltpu.CompilerParams(
            collective_id=0, has_side_effects=True, vmem_limit_bytes=64 << 20
        ),
    )(*args)
    coarse, grad_conv, grad_down = pl.pallas_call(
        finish,
        out_shape=[
            jax.ShapeDtypeStruct(cotangent.shape, BF16),
            jax.ShapeDtypeStruct((offsets * width, width), F32),
            jax.ShapeDtypeStruct((OCT * width, 256), F32),
        ],
        in_specs=[hbm] * 4,
        out_specs=[hbm] * 3,
        scratch_shapes=[
            *[pltpu.VMEM(part.shape, BF16) for part in parts[1:]],
            pltpu.VMEM((offsets * width, width), F32),
            pltpu.VMEM((OCT * width, 256), F32),
            pltpu.SemaphoreType.DMA((3, 2)),
            pltpu.SemaphoreType.DMA((3, 2)),
        ],
        compiler_params=pltpu.CompilerParams(vmem_limit_bytes=64 << 20),
    )(*parts)
    return (coarse, grad_conv.reshape(offsets, width, width), grad_down)


def solution(mesh):
    n, nx = math.isqrt(mesh.shape["blk"] // 2), mesh.shape["dp"]
    in_specs = (
        P("dp", "blk", None),
        P("dp", None, "blk"),
        P("dp", None),
        P("dp", "blk"),
        P("dp", "blk"),
        P(),
        P(),
        P("dp", "blk", None),
    )
    out_specs = (P("dp", "blk", None), P(), P())
    return jax.shard_map(
        functools.partial(body, n, nx),
        mesh=mesh,
        in_specs=in_specs,
        out_specs=out_specs,
        check_vma=False,
    )
```

```python
import functools
import math

import jax
import jax.numpy as jnp
from jax import lax
from jax.experimental import pallas as pl
from jax.experimental.pallas import tpu as pltpu
from jax.sharding import PartitionSpec as P

OCT = 8
HALO = 64
F32 = jnp.float32
BF16 = jnp.bfloat16
MESH = pl.DeviceIdType.MESH


def iota(shape, dim):
    return lax.broadcasted_iota(jnp.int32, shape, dim)


def dot(a, b, ca, cb):
    return lax.dot_general(a, b, (((ca,), (cb,)), ((), ())), preferred_element_type=F32)


def up16(rows):
    return -(-rows // 16) * 16


def far_first(n):
    return sorted(range(1, n), key=lambda p: -min(p, n - p))


class Place:
    def __init__(self, n, nx):
        blk = lax.axis_index("blk")
        self.n, self.nx = n, nx
        self.blk, self.x = blk, lax.axis_index("dp")
        self.c = lax.rem(blk, 2)
        chip = lax.div(blk, 2)
        z, y = lax.div(chip, n), lax.rem(chip, n)
        self.a = (1 - self.c) * y + self.c * z
        self.b = (1 - self.c) * z + self.c * y

    def of(self, a, b):
        c, n = self.c, self.n
        return ((1 - c) * (b * n + a) + c * (a * n + b)) * 2 + c

    def axis(self, name):
        if name == "x":
            return self.nx, self.x, self.along_x
        return (self.n, self.a, self.along_a) if name == "a" else (self.n, self.b, self.along_b)

    def along_a(self, p):
        return (self.of(lax.rem(self.a + p, self.n), self.b), self.x)

    def along_b(self, p):
        return (self.of(self.a, lax.rem(self.b + p, self.n)), self.x)

    def along_x(self, p):
        return (self.blk, lax.rem(self.x + p, self.nx))

    def other_core(self):
        return (self.blk + 1 - 2 * self.c, self.x)

    def next_block(self, p, count):
        return (lax.rem(self.blk + p, count), self.x)


class Sender:
    def __init__(self, send_sem, recv_sem):
        self.send_sem, self.recv_sem, self.used, self.all = send_sem, recv_sem, 0, []

    def start(self, src, dst, device):
        copy = pltpu.make_async_remote_copy(
            src_ref=src,
            dst_ref=dst,
            send_sem=self.send_sem.at[self.used],
            recv_sem=self.recv_sem.at[self.used],
            device_id=device,
            device_id_type=MESH,
        )
        self.used += 1
        copy.start()
        self.all.append(copy)
        return copy

    def finish(self, recent=0):
        old = len(self.all) - recent
        for copy in self.all[:old]:
            copy.wait_send()
        self.all = self.all[old:]


def arrived(copies):
    for copy in copies:
        copy.wait_recv()


class Exchange:
    def __init__(self, place, sender, bufs, whole):
        self.place, self.sender, self.whole = place, sender, whole
        self.send1, self.recv1, self.send2, self.recv2, self.got = bufs
        if whole:
            self.recv2 = self.got.at[place.c]

    def start(self, rows):
        pc, n = self.place, self.place.n
        self.send1[...] = rows.reshape(self.send1.shape)
        self.copies = [
            self.sender.start(
                self.send1.at[lax.rem(pc.a + p, n)], self.recv1.at[pc.a], pc.along_a(p)
            )
            for p in far_first(n)
        ]
        self.recv1[pc.a] = self.send1[pc.a]

    def second(self, swap):
        pc, n = self.place, self.place.n
        arrived(self.copies)
        flat = self.recv1[...].reshape(swap.shape[1], -1)
        moved = jnp.dot(swap[...], flat, preferred_element_type=F32).astype(BF16)
        self.send2[...] = moved.reshape(self.send2.shape)
        self.copies = [
            self.sender.start(
                self.send2.at[lax.rem(pc.b + p, n)], self.recv2.at[pc.b], pc.along_b(p)
            )
            for p in far_first(n)
        ]
        self.recv2[pc.b] = self.send2[pc.b]

    def third(self):
        pc = self.place
        arrived(self.copies)
        if self.whole:
            self.copies = [self.sender.start(self.recv2, self.recv2, pc.other_core())]
            return
        self.copies = [
            self.sender.start(self.recv2.at[:, 1 - pc.c], self.got.at[pc.c], pc.other_core())
        ]
        self.got[pc.c] = self.recv2[:, pc.c]

    def result(self):
        arrived(self.copies)
        if self.whole:
            rows = [self.got[:, :, core] for core in range(2)]
            return [flat.reshape(-1, flat.shape[-1]) for flat in rows]
        flat = self.got[...]
        return flat.reshape(-1, flat.shape[-1])


class Sum:
    def __init__(self, place, sender, rows, order, bufs, out):
        self.place, self.sender, self.out = place, sender, out
        self.axes = [place.axis(name) for name in order]
        self.rows, self.part, self.wide = self.sizes(rows, *[axis[0] for axis in self.axes[:2]])
        self.own, self.s1, self.r1, self.s2, self.r2, self.s3, self.g2, self.g1 = bufs

    @staticmethod
    def sizes(rows, n1, n2):
        chunk = rows // n1
        return chunk, up16(-(-chunk // n2)), up16(chunk)

    @staticmethod
    def scratch(rows, n1, n2, n3, middle):
        _, part, wide = Sum.sizes(rows, n1, n2)
        return [
            pltpu.VMEM((rows, 128), F32),
            pltpu.VMEM((n1, wide, 128), BF16),
            pltpu.VMEM((n1, wide, 128), BF16),
            pltpu.VMEM((n2, part, 128), middle),
            pltpu.VMEM((n2, part, 128), middle),
            pltpu.VMEM((n3, part, 128), middle),
            pltpu.VMEM((n2 * part, 128), BF16),
            pltpu.VMEM((n1, wide, 128), BF16),
        ]

    def first(self):
        (n, me, along), rows = self.axes[0], self.rows
        self.copies = []
        for p in far_first(n):
            q = lax.rem(me + p, n)
            chunk = self.own[pl.ds(pl.multiple_of(q * rows, 8), rows)]
            self.s1[q, pl.ds(0, rows)] = chunk.astype(BF16)
            if self.wide > rows:
                self.s1[q, pl.ds(rows, self.wide - rows)] = jnp.zeros(
                    (self.wide - rows, 128), BF16
                )
            self.copies.append(self.sender.start(self.s1.at[q], self.r1.at[p], along(p)))

    def second(self):
        (n1, me1, _), (n, me, along), rows = self.axes[0], self.axes[1], self.rows
        arrived(self.copies)
        total = self.own[pl.ds(pl.multiple_of(me1 * rows, 8), rows)]
        for p in range(1, n1):
            total += self.r1[p][:rows].astype(F32)
        spare = n * self.part - rows
        if spare:
            total = jnp.concatenate([total, jnp.zeros((spare, 128), F32)], 0)
        self.s2[...] = total.reshape(self.s2.shape).astype(self.s2.dtype)
        self.copies = [
            self.sender.start(self.s2.at[lax.rem(me + p, n)], self.r2.at[p], along(p))
            for p in far_first(n)
        ]

    def third(self):
        (n2, me2, _), (n, me, along) = self.axes[1:]
        arrived(self.copies)
        total = self.s2[me2].astype(F32)
        for p in range(1, n2):
            total += self.r2[p].astype(F32)
        self.s3[me] = total.astype(self.s3.dtype)
        self.copies = [
            self.sender.start(self.s3.at[me], self.s3.at[me], along(p)) for p in far_first(n)
        ]

    def back_second(self):
        n, me, along = self.axes[1]
        arrived(self.copies)
        total = self.s3[0].astype(F32)
        for x in range(1, self.axes[2][0]):
            total += self.s3[x].astype(F32)
        mine = pl.ds(pl.multiple_of(me * self.part, 16), self.part)
        self.g2[mine] = total.astype(BF16)
        self.copies = [
            self.sender.start(self.g2.at[mine], self.g2.at[mine], along(p)) for p in far_first(n)
        ]

    def back_first(self):
        n, me, along = self.axes[0]
        arrived(self.copies)
        self.g1[me] = self.g2[pl.ds(0, self.wide)]
        self.copies = [
            self.sender.start(self.g1.at[me], self.g1.at[me], along(p)) for p in far_first(n)
        ]

    def back_core(self, sem):
        pc = self.place
        arrived(self.copies)
        self.copies = [self.sender.start(self.g1, self.out.at[pc.c], pc.other_core())]
        self.kept = pltpu.make_async_copy(self.g1, self.out.at[pc.c], sem)
        self.kept.start()

    def result(self):
        arrived(self.copies)
        self.kept.wait()


def conv_split(rows):
    return rows * 13 // 27


ORDERS = (("a", "b", "x"), ("x", "a", "b"), ("x", "a", "b"))


def kernel(n, nx, cap, *refs):
    given, (out_coarse, *outs), refs = refs[:8], refs[8:12], refs[12:]
    (
        kernel_map,
        block_counts,
        send_position,
        conv_weight,
        down_weight,
        cell_source,
        cotangent,
        raw,
        weight_t,
        picked,
        by_child,
        send_hot,
        swap,
        coarse,
        their_raw,
        their_map,
        their_picked,
        grad_pre,
        *rest,
    ) = refs
    *rest, send_sem, recv_sem, local_sem, load_sem = rest
    count = 2 * n * n
    features = given[0]
    offsets = conv_weight.shape[0]
    rows, width = features.shape[1], features.shape[2]
    cells = count * cap
    half = offsets * width // 2
    pc = Place(n, nx)
    sender = Sender(send_sem, recv_sem)

    barrier = pltpu.get_barrier_semaphore()
    partners = [pc.along_a(p) for p in range(1, n)] + [pc.along_b(p) for p in range(1, n)]
    partners += [pc.along_x(p) for p in range(1, nx)]
    partners += [pc.other_core(), pc.next_block(1, count), pc.next_block(count - 1, count)]
    for device in partners:
        pl.semaphore_signal(barrier, inc=1, device_id=device, device_id_type=MESH)

    sources = [features.at[0], *given[1:7], given[7].at[0]]
    targets = [raw.at[pl.ds(HALO, rows)], kernel_map, block_counts, send_position]
    targets += [cell_source.at[pc.c], conv_weight, down_weight, cotangent.at[pc.c]]
    loads = [
        pltpu.make_async_copy(src, dst, load_sem.at[i])
        for i, (src, dst) in enumerate(zip(sources, targets))
    ]
    for i in (7, 6, 4, 0, 2, 3, 1, 5):
        loads[i].start()
    pl.semaphore_wait(barrier, len(partners))

    halo = [
        sender.start(
            features.at[0, pl.ds(rows - HALO, HALO)],
            raw.at[pl.ds(0, HALO)],
            pc.next_block(1, count),
        ),
        sender.start(
            features.at[0, pl.ds(0, HALO)],
            raw.at[pl.ds(HALO + rows, HALO)],
            pc.next_block(count - 1, count),
        ),
    ]
    shared = [
        sender.start(given[4], cell_source.at[pc.c], pc.other_core()),
        sender.start(given[7].at[0], cotangent.at[pc.c], pc.other_core()),
    ]
    shared_map = sender.start(given[1], their_map, pc.other_core())

    forward = Exchange(pc, sender, rest[0:5], True)
    backward = Exchange(pc, sender, rest[5:10], False)
    first_rows = conv_split(half)
    sums = [
        Sum(pc, sender, total, order, rest[10 + 8 * i : 18 + 8 * i], outs[i])
        for i, (total, order) in enumerate(
            zip((first_rows, half - first_rows, OCT * width), ORDERS)
        )
    ]
    sum_conv, sum_down = sums[:2], sums[2]

    r = iota((cells, 1), 0)
    slot, r1 = lax.rem(r, cap), lax.div(r, cap)
    to_b, r2 = lax.rem(r1, n), lax.div(r1, n)
    to_c, to_a = lax.rem(r2, 2), lax.div(r2, 2)
    chip = jnp.where(pc.c == 0, to_b * n + to_a, to_a * n + to_b)
    goes_to = (chip * 2 + to_c) * cap + slot
    from_a, from_b, from_c = to_b, lax.rem(r2, n), lax.div(r2, n)
    chip = jnp.where(from_c == 0, from_b * n + from_a, from_a * n + from_b)
    comes_from = (chip * 2 + from_c) * cap + slot

    def hot(at, values):
        return jnp.where(at == values, 1.0, 0.0).astype(BF16)

    for i in (7, 6, 4):
        loads[i].wait()
    for j in range(OCT):
        part = dot(cotangent[pc.c], down_weight[pl.ds(j * width, width)], 1, 1)
        by_child[0, pl.ds(j, rows // 4, stride=OCT)] = part.astype(BF16).astype(F32)
    backward.start(
        jnp.dot(
            hot(goes_to, cell_source[pc.c]),
            by_child[0].astype(BF16),
            preferred_element_type=F32,
        ).astype(BF16)
    )

    loads[0].wait()
    loads[2].wait()

    def live_of(block, inside):
        counted = block_counts[0, lax.rem(block, count)]
        front = lax.div(counted, 2)
        return (inside < front) | (inside >= rows - (counted - front))

    loads[5].wait()
    for k in range(offsets):
        weight_t[:, pl.ds(k * width, width)] = conv_weight[k].astype(F32).T.astype(BF16)
    loads[1].wait()
    lane = lax.rem(iota((1, rows), 1), 128)
    window = iota((2 * HALO + 128, 128), 0)
    live_t = live_of(pc.blk, iota((1, rows), 1))

    def table_of(block, ref):
        live = jnp.concatenate(
            [
                live_of(block + count - 1, iota((HALO, width), 0) + rows - HALO),
                live_of(block, iota((rows, width), 0)),
                live_of(block + 1, iota((HALO, width), 0)),
            ],
            0,
        )
        return jnp.where(live, ref[...].astype(F32), 0.0).T.astype(BF16)

    def pick(table_t, entry, k, ref):
        index = jnp.where(entry >= 0, entry + lane, -1)
        for t in range(rows // 128):
            chosen = hot(window, index[:, t * 128 : (t + 1) * 128])
            got = jnp.dot(
                table_t[:, t * 128 : t * 128 + 128 + 2 * HALO], chosen, preferred_element_type=F32
            )
            ref[pl.ds(k * width, width), pl.ds(t * 128, 128)] = got.astype(BF16)

    arrived(halo)
    shared_raw = sender.start(raw, their_raw, pc.other_core())
    table_t = table_of(pc.blk, raw)
    for k in range(offsets):
        pick(table_t, kernel_map[k], k, picked)

    loads[3].wait()
    position = send_position[...]
    send_hot[...] = hot(goes_to, position)
    pre = jnp.dot(weight_t[...], picked[...], preferred_element_type=F32)
    sig = 1.0 / (1.0 + jnp.exp(-pre))
    hidden = jnp.where(live_t, pre * sig, 0.0).astype(BF16)
    forward.start(dot(send_hot[...], hidden, 1, 1).astype(BF16))

    swapped = ((to_b * 2 + to_c) * n + to_a) * cap + slot
    swap[...] = hot(swapped, iota((1, cells), 1))
    backward.second(swap)
    from_owner = hot(comes_from, position)
    slope = jnp.where(live_t, sig * (1.0 + pre * (1.0 - sig)), 0.0)

    arrived([shared_map, shared_raw])
    skipped = offsets // 2
    table_t = table_of(pc.blk + 1 - 2 * pc.c, their_raw)
    for k in range(offsets - skipped):
        pick(table_t, their_map[pc.c * skipped + k], k, their_picked)

    forward.second(swap)
    backward.third()
    grad_hidden = dot(backward.result(), from_owner, 0, 0)
    grad_pre[pc.c] = (grad_hidden * slope).astype(BF16)
    shared_grad = sender.start(grad_pre.at[pc.c], grad_pre.at[pc.c], pc.other_core())
    splits = (
        (sum_conv[0], 0, first_rows),
        (sum_conv[1], first_rows, half - first_rows),
    )
    for job, start, size in splits:
        mine = picked[pl.ds(pl.multiple_of(pc.c * half + start, 16), size)]
        job.own[...] = dot(mine, grad_pre[pc.c], 1, 1)
    arrived([shared_grad])
    for job, start, size in splits:
        at = pc.c * (half - skipped * width) + start
        theirs = their_picked[pl.ds(pl.multiple_of(at, 16), size)]
        job.own[...] += dot(theirs, grad_pre[1 - pc.c], 1, 1)
        job.first()
    forward.third()

    arrived(shared)
    for core, incoming in enumerate(forward.result()):
        by_child[core] = dot(hot(comes_from, cell_source[core]), incoming, 0, 0)
    quarter = rows // 4
    mine = pl.ds(pl.multiple_of(pc.c * 128, 128), 128)
    wanted = jnp.concatenate([cotangent[core, :, mine] for core in range(2)], 0)
    for j in range(OCT):
        child = [by_child[core, pl.ds(j, quarter, stride=OCT)] for core in range(2)]
        child = jnp.concatenate(child, 0).astype(BF16)
        sum_down.own[pl.ds(j * width, width)] = dot(child, wanted, 0, 0)
    sum_down.first()
    total = jnp.zeros(coarse.shape[1:], F32)
    for j in range(OCT):
        child = by_child[pc.c, pl.ds(j, quarter, stride=OCT)].astype(BF16)
        total += jnp.dot(
            child, down_weight[pl.ds(j * width, width)], preferred_element_type=F32
        )
    coarse[0] = total.astype(BF16)
    kept = pltpu.make_async_copy(coarse, out_coarse, local_sem.at[3])
    kept.start()

    for job in sums:
        job.second()
    for job in sums:
        job.third()
    for job in sums:
        job.back_second()
    sent = len(sender.all)
    for job in sums:
        job.back_first()
    sender.finish(len(sender.all) - sent)
    for i, job in enumerate(sums):
        job.back_core(local_sem.at[i])
    kept.wait()
    sender.finish(len(sums))
    for job in sums:
        job.result()
    sender.finish()


def finish(coarse, conv_a, conv_x, down, out_coarse, out_conv, out_down, *refs):
    *stored, full_conv, full_down, load_sem, save_sem = refs
    given = (conv_a, conv_x, down)
    half = out_conv.shape[0] // 2
    first_rows = conv_split(half)
    loads = [
        [pltpu.make_async_copy(src.at[h], dst.at[h], load_sem.at[i, h]) for h in range(2)]
        for i, (src, dst) in enumerate(zip(given, stored))
    ]
    for i in range(3):
        for h in range(2):
            loads[i][h].start()
    saves = [pltpu.make_async_copy(coarse, out_coarse, save_sem.at[2, 1])]
    saves[0].start()
    for i, start, rows in ((0, 0, first_rows), (1, first_rows, half - first_rows)):
        for h in range(2):
            loads[i][h].wait()
            n = stored[i].shape[1]
            chunk = rows // n
            for q in range(n):
                full_conv[pl.ds(h * half + start + q * chunk, chunk)] = stored[i][
                    h, q, pl.ds(0, chunk)
                ].astype(F32)
            at = pl.ds(h * half + start, rows)
            saves.append(
                pltpu.make_async_copy(full_conv.at[at], out_conv.at[at], save_sem.at[i, h])
            )
            saves[-1].start()
    for h in range(2):
        loads[2][h].wait()
        full_down[:, pl.ds(h * 128, 128)] = (
            stored[2][h].reshape(full_down.shape[0], 128).astype(F32)
        )
    saves.append(pltpu.make_async_copy(full_down, out_down, save_sem.at[2, 0]))
    saves[-1].start()
    for save in saves:
        save.wait()


def body(n, nx, *args):
    args = list(args)
    args[1] = jnp.transpose(args[1], (1, 0, 2))
    features, _, _, _, cell_source, conv_weight, _, cotangent = args
    rows, width = features.shape[1:]
    offsets = conv_weight.shape[0]
    cells = cell_source.shape[1]
    cap = cells // (2 * n * n)
    half = offsets * width // 2
    first_rows = conv_split(half)
    exchange = [
        pltpu.VMEM((n, cells // n, width), BF16),
        pltpu.VMEM((n, cells // n, width), BF16),
        pltpu.VMEM((n, 2, cells // n // 2, width), BF16),
        pltpu.VMEM((n, 2, cells // n // 2, width), BF16),
    ]
    one = pltpu.VMEM((2, n, cells // n // 2, width), BF16)
    both = pltpu.VMEM((2, n, 2, cells // n // 2, width), BF16)
    sizes = {"a": n, "b": n, "x": nx}
    jobs = [
        (total, *[sizes[name] for name in order])
        for total, order in zip((first_rows, half - first_rows, OCT * width), ORDERS)
    ]
    copies = 7 + 2 * (2 * (n - 1) + 1)
    copies += sum(1 + 2 * (n1 - 1) + 2 * (n2 - 1) + n3 - 1 for _, n1, n2, n3 in jobs)
    hbm = pl.BlockSpec(memory_space=pl.ANY)
    parts = pl.pallas_call(
        functools.partial(kernel, n, nx, cap),
        out_shape=[jax.ShapeDtypeStruct(cotangent.shape, BF16)]
        + [
            jax.ShapeDtypeStruct((2, n1, up16(total // n1), 128), BF16) for total, n1, _, _ in jobs
        ],
        in_specs=[hbm] * 8,
        out_specs=[hbm] * 4,
        scratch_shapes=[
            *[
                (pltpu.SMEM if i == 2 else pltpu.VMEM)(args[i].shape, args[i].dtype)
                for i in (1, 2, 3, 5, 6)
            ],
            pltpu.VMEM((2, 1, cells), jnp.int32),
            pltpu.VMEM((2, *cotangent.shape[1:]), BF16),
            pltpu.VMEM((rows + 2 * HALO, width), BF16),
            pltpu.VMEM((width, offsets * width), BF16),
            pltpu.VMEM((offsets * width, rows), BF16),
            pltpu.VMEM((2, cells, width), F32),
            pltpu.VMEM((cells, rows), BF16),
            pltpu.VMEM((cells, cells), BF16),
            pltpu.VMEM(cotangent.shape, BF16),
            pltpu.VMEM((rows + 2 * HALO, width), BF16),
            pltpu.VMEM(args[1].shape, jnp.int32),
            pltpu.VMEM(((offsets - offsets // 2) * width, rows), BF16),
            pltpu.VMEM((2, width, rows), BF16),
            *exchange,
            both,
            *exchange,
            one,
            *[
                ref
                for job, order in zip(jobs, ORDERS)
                for ref in Sum.scratch(*job, BF16 if order[0] == "x" else F32)
            ],
            pltpu.SemaphoreType.DMA((copies,)),
            pltpu.SemaphoreType.DMA((copies,)),
            pltpu.SemaphoreType.DMA((4,)),
            pltpu.SemaphoreType.DMA((8,)),
        ],
        compiler_params=pltpu.CompilerParams(
            collective_id=0, has_side_effects=True, vmem_limit_bytes=64 << 20
        ),
    )(*args)
    coarse, grad_conv, grad_down = pl.pallas_call(
        finish,
        out_shape=[
            jax.ShapeDtypeStruct(cotangent.shape, BF16),
            jax.ShapeDtypeStruct((offsets * width, width), F32),
            jax.ShapeDtypeStruct((OCT * width, 256), F32),
        ],
        in_specs=[hbm] * 4,
        out_specs=[hbm] * 3,
        scratch_shapes=[
            *[pltpu.VMEM(part.shape, BF16) for part in parts[1:]],
            pltpu.VMEM((offsets * width, width), F32),
            pltpu.VMEM((OCT * width, 256), F32),
            pltpu.SemaphoreType.DMA((3, 2)),
            pltpu.SemaphoreType.DMA((3, 2)),
        ],
        compiler_params=pltpu.CompilerParams(vmem_limit_bytes=64 << 20),
    )(*parts)
    return (coarse, grad_conv.reshape(offsets, width, width), grad_down)


def solution(mesh):
    n, nx = math.isqrt(mesh.shape["blk"] // 2), mesh.shape["dp"]
    in_specs = (
        P("dp", "blk", None),
        P("dp", None, "blk"),
        P("dp", None),
        P("dp", "blk"),
        P("dp", "blk"),
        P(),
        P(),
        P("dp", "blk", None),
    )
    out_specs = (P("dp", "blk", None), P(), P())
    return jax.shard_map(
        functools.partial(body, n, nx),
        mesh=mesh,
        in_specs=in_specs,
        out_specs=out_specs,
        check_vma=False,
    )
```
